32 devices in a mesh: groups: 2 (over x), ctx: 16 (over z, y, core).
Axes of the slice: x: 2, y: 2, z: 4, core: 2. Of those that a mesh axis runs over, the one named last changes fastest.
Arguments:
- queries: bfloat16 [256, 2048], P(('groups', 'ctx')), parts along dimension 0, may hold values from -8 to 8, as said below
- keys: bfloat16 [2, 8192, 256], P('groups', 'ctx'), parts along dimension 0, may hold values from -8 to 8
- values: bfloat16 [2, 8192, 256], P('groups', 'ctx'), parts along dimension 0, may hold values from -16 to 16
- lengths: int32 [2], P('groups'), parts along dimension 0, may hold values from 4096 to 8192, as said below
- owner_counts: int32 [32], P('groups'), parts along dimension 0, may hold values from 1 to 16, 128 in all
- row_order: int32 [256], P('groups'), parts along dimension 0, may hold values from 0 to 127, each once
- residual: bfloat16 [512, 2048], P(('groups', 'ctx')), parts along dimension 0, may hold values from -40 to 40, as said below
- out_weight: bfloat16 [2048, 2048], P('ctx'), may hold values from -0.125 to 0.125
- norm_gain: float32 [2048], replicated, may hold values from 0.1 to 1.9
- expert_ids: int32 [512, 8], P(('groups', 'ctx')), parts along dimension 0, may hold values from 0 to 15, all different within a row; in each aligned block of 16 rows (0 to 15, 16 to 31, ...) at most 16 rows name the same one
- route_weights: float32 [512, 8], P(('groups', 'ctx')), parts along dimension 0, may hold values from 0.1 to 1
- gate_up: bfloat16 [16, 2048, 1536], P('ctx'), may hold values from -0.125 to 0.125
- expert_down: bfloat16 [16, 768, 2048], P('ctx'), may hold values from -0.21875 to 0.21875
Outputs:
- attn_slots: bfloat16 [512, 2048], P(('groups', 'ctx')), parts along dimension 0
- layer_out: bfloat16 [512, 2048], P(('groups', 'ctx')), parts along dimension 0
The draws below stay inside these ranges and needn't reach their ends.
There are 2 independent parts, one for each index of `groups`. The reference program is written for one: setup_inputs(seed, part) draws one part's arguments, and reference() takes and returns one part's arrays. A program takes and returns all parts, laid end to end along the dimension named above; an argument that names none is the same for every part. Nothing has to cross between parts.
Inputs may be any that keep to these rules, and one draw needn't show every extreme that they name: Large entries of queries and keys may line up. `lengths`: at least 4096; one request has exactly 8192. `owner_counts`: sum to 128; the largest is exactly 16. `row_order`: each row once. `residual`: entries may be any real values in the range. `expert_ids`: each slot names 8 different experts; within the 16 slots of one owner no expert is named more than 16 times, and some expert exactly that many times.
All inputs are finite; a program needn't handle non-finite values.
Results may differ from the reference program's by a relative error of at most 0.009.
Values may be sent and summed in bfloat16 or wider, within the bound.
A program may use at most 128 MiB of HBM per device.

```python
import math
import jax
import jax.numpy as jnp
import numpy as np
from jax import lax

D = 2048
HQ = 16
KVH = 2
HD = 128
EFF = 768
TOPK = 8
STRETCH = 128
CACHE_DEV = 512
ROWS = 128
REQS = 1
CTX_LEN = 8192
CAP_ROWS = 16
SLOTS = 256
EXPERTS = 16
ROUTE_CAP = 16
N_CTX = 16


def quiet_blocks(key):
    quarter = max(1, N_CTX // 4)
    picks_count = min(4, quarter)
    request_keys = jax.random.split(jax.random.fold_in(key, 7001), REQS)

    def one_order(one_key):
        return jax.random.permutation(one_key, quarter)
    orders = jax.vmap(one_order)(request_keys)
    chosen = orders[:, :picks_count].astype(jnp.int32)
    block_of = (jnp.arange(CTX_LEN, dtype=jnp.int32) // CACHE_DEV).astype(jnp.int32)
    return jnp.any(block_of[None, :, None] == chosen[:, None, :], axis=-1)


def draw_queries(key, part):
    drawn = jnp.clip(jax.random.normal(jax.random.fold_in(key, 11), (ROWS, HQ * HD), jnp.float32) * 1.6, -8.0, 8.0)
    return drawn.astype(jnp.bfloat16)


def draw_keys(key, part):
    drawn = jnp.clip(jax.random.normal(jax.random.fold_in(key, 21), (REQS, CTX_LEN, KVH * HD), jnp.float32) * 2.0, -8.0, 8.0)
    softer = jax.random.normal(jax.random.fold_in(key, 24), (REQS, CTX_LEN, KVH * HD), jnp.float32) * 0.25
    silent = quiet_blocks(key)
    drawn = jnp.where(silent[..., None], jnp.clip(softer, -8.0, 8.0), drawn)
    return drawn.astype(jnp.bfloat16)


def draw_values(key, part):
    silent = quiet_blocks(key)
    polarity = jnp.where(jax.random.bernoulli(jax.random.fold_in(key, 51), 0.5, (REQS, 1, KVH * HD)), 1.0, -1.0)
    magnitude = jax.random.uniform(jax.random.fold_in(key, 54), (REQS, CTX_LEN, KVH * HD), jnp.float32, 10.0, 14.0)
    entries = jnp.clip(jax.random.normal(jax.random.fold_in(key, 55), (REQS, CTX_LEN, KVH * HD), jnp.float32) * 0.15, -1.0, 1.0)
    drawn = jnp.where(silent[..., None], polarity * magnitude, entries)
    return jnp.clip(drawn, -16.0, 16.0).astype(jnp.bfloat16)


def draw_lengths(key, part):
    drawn = jax.random.randint(jax.random.fold_in(key, 31), (REQS,), CTX_LEN // 2, CTX_LEN + 1)
    which = jax.random.randint(jax.random.fold_in(key, 32), (), 0, REQS)
    return jnp.where(jnp.arange(REQS) == which, CTX_LEN, drawn).astype(jnp.int32)


def draw_residual(key, part):
    row_scale = jnp.exp(jax.random.uniform(jax.random.fold_in(key, 41), (SLOTS, 1), jnp.float32, jnp.log(0.3), jnp.log(3.0)))
    col_scale = jnp.exp(jax.random.uniform(jax.random.fold_in(key, 42), (1, D), jnp.float32, jnp.log(0.3), jnp.log(3.0)))
    drawn = row_scale * col_scale * jnp.clip(jax.random.normal(jax.random.fold_in(key, 45), (SLOTS, D), jnp.float32), -4.0, 4.0)
    return jnp.clip(drawn, -40.0, 40.0).astype(jnp.bfloat16)


def block_levels(own_key, shape, cuts, least, top_value):
    level = 1.0
    for position, parts in cuts:
        draws = jax.random.uniform(jax.random.fold_in(jax.random.fold_in(own_key, 6), position), (parts,), jnp.float32, least / len(cuts), top_value / len(cuts))
        level = level * jnp.repeat(jnp.exp(draws), shape[position] // parts).reshape((-1,) + (1,) * (len(shape) - 1 - position))
    return level


def profile(count, total, reach, slope):
    loads = [(1 << 20) // math.isqrt(standing ** slope) + 1 for standing in range(2, count + 1)]
    spare, given = total - reach - (count - 1), [1] * (count - 1)
    while spare > 0:
        free = [i for i in range(count - 1) if given[i] < reach]
        mass, remaining = sum([loads[i] for i in free]), spare
        for i in free:
            extra = min(reach - given[i], max(1, remaining * loads[i] // mass), spare)
            given[i] = given[i] + extra
            spare = spare - extra
    return np.array([reach] + given)


def uneven(rng, count, total, reach, slope):
    if count == 2:
        one = jax.random.randint(rng, (), max(1, total - reach), min(reach, total - 1) + 1)
        return jnp.stack([one, total - one])
    sizes = jnp.asarray(profile(count, total, reach, slope), jnp.int32)
    couples = (count - 1) // 2
    source_of, taker = sizes[1:1 + 2 * couples:2], sizes[2:2 + 2 * couples:2]
    margin = jnp.minimum(source_of - 1, reach - taker)
    shifted = jax.random.randint(jax.random.fold_in(rng, 1), (couples,), 0, 1 << 20) % (margin + 1)
    sizes = sizes.at[1:1 + 2 * couples:2].set(source_of - shifted).at[2:2 + 2 * couples:2].set(taker + shifted)
    return sizes[jax.random.permutation(jax.random.fold_in(rng, 2), count)]


def assign_block(key, own, number, rows, count, top, reach, slope):
    ranking = jax.random.permutation(key, count)
    packed, usual = load_shares(count, rows * top, reach, slope, True), load_shares(count, rows * top, reach, slope, False)
    places = jnp.arange(count)

    def named(tallies, offset_by):
        used = int((tallies > 0).sum())
        fixed = max(1, used // 4)
        moved = fixed + (places - fixed + offset_by * (used - fixed)) % max(1, count - fixed)
        return jnp.zeros((count,), jnp.int32).at[ranking[jnp.where(places < fixed, places, moved)]].set(jnp.asarray(tallies, jnp.int32))

    tallies = jnp.where(number % 4 == 0, named(packed, number // 4), named(usual, number - number // 4 - 1))
    mixed = jax.random.permutation(jax.random.fold_in(own, 3), count)
    giver, sink = mixed[0:count // 2 * 2:2], mixed[1:count // 2 * 2:2]
    slack = jnp.minimum(tallies[giver] - 1, reach - tallies[sink]) // 2
    slack = jnp.where((giver == ranking[0]) | (sink == ranking[0]) | (tallies[sink] == 0), 0, jnp.maximum(slack, 0))
    moved = jax.random.randint(jax.random.fold_in(own, 4), (count // 2,), 0, 1 << 20) % (slack + 1)
    tallies = tallies.at[giver].add(-moved).at[sink].add(moved)
    items = jnp.searchsorted(jnp.cumsum(tallies), jnp.arange(rows * top), side="right").astype(jnp.int32)
    listing = items.reshape(top, rows).T
    listing = listing[jax.random.permutation(jax.random.fold_in(own, 1), rows)]
    offset_by = jax.random.randint(jax.random.fold_in(own, 2), (rows, 1), 0, top)
    return jnp.take_along_axis(listing, (jnp.arange(top)[None, :] + offset_by) % top, axis=1)


def load_shares(number_of, total, limit, slope, full):
    loads = [(1 << 20) // math.isqrt(grade ** slope) + 1 for grade in range(1, number_of + 1)]
    largest = limit if full else min(limit, max(-(-total // number_of), total * loads[0] // sum(loads)))
    least = 1 if total - largest >= number_of - 1 else 0
    holding, rest = [largest] + [least] * (number_of - 1), total - largest - least * (number_of - 1)
    while rest > 0:
        free = [i for i in range(1, number_of) if holding[i] < largest] or [i for i in range(1, number_of) if holding[i] < limit]
        whole, remaining = sum([loads[i] for i in free]), rest
        for i in free:
            more = min(limit - holding[i], max(1, remaining * loads[i] // whole), rest)
            holding[i] = holding[i] + more
            rest = rest - more
    return np.array(holding)


def gaussian(stream_key, shape, width, limit, shards=(), kind=jnp.bfloat16):
    array = jax.random.normal(stream_key, shape, jnp.float32) * width
    if len(shards) > 0:
        array = block_levels(stream_key, shape, shards, -0.22, 0.18) * array
    return jnp.clip(array, min=-limit, max=limit).astype(kind)


def setup_inputs(seed: int = 0, part: int = 0) -> dict:
    streams_of = jax.random.split(jax.random.key(seed), 14)
    part_keys = jax.random.split(jax.random.fold_in(streams_of[13], part), 14)
    queries = draw_queries(jax.random.fold_in(jax.random.fold_in(streams_of[13], part), 71), part)
    keys = draw_keys(jax.random.fold_in(jax.random.fold_in(streams_of[13], part), 71), part)
    values = draw_values(jax.random.fold_in(jax.random.fold_in(streams_of[13], part), 71), part)
    lengths = draw_lengths(jax.random.fold_in(jax.random.fold_in(streams_of[13], part), 71), part)
    owner_counts = uneven(part_keys[4], N_CTX, ROWS, CAP_ROWS, 2).astype(jnp.int32)
    row_order = jax.random.permutation(part_keys[5], ROWS).astype(jnp.int32)
    residual = draw_residual(jax.random.fold_in(jax.random.fold_in(streams_of[13], part), 71), part)
    out_weight = gaussian(streams_of[7], (HQ * HD, D), (HQ * HD) ** -0.5, 0.125, ((0, 16),))
    norm_gain = jnp.clip(1.0 + 0.18 * jax.random.normal(streams_of[8], (D,), jnp.float32), 0.1, 1.9)
    expert_ids_keys = jax.random.split(jax.random.fold_in(part_keys[9], 1), SLOTS // CAP_ROWS)
    expert_ids_turns = jax.random.permutation(jax.random.fold_in(part_keys[9], 3), SLOTS // CAP_ROWS)
    expert_ids = jax.vmap(lambda own, number: assign_block(jax.random.fold_in(part_keys[9], 2), own, number, CAP_ROWS, EXPERTS, TOPK, ROUTE_CAP, 2))(expert_ids_keys, expert_ids_turns).reshape((SLOTS, TOPK))
    route_weights = jnp.clip(jnp.exp(math.log(1.0) - 2.3025851 * jax.random.uniform(part_keys[10], (SLOTS, TOPK), jnp.float32) ** block_levels(part_keys[10], (SLOTS, TOPK), ((0, 16),), -0.2, 0.2)), 0.1, 1.0)
    gate_up = gaussian(streams_of[11], (EXPERTS, D, 2 * EFF), D ** -0.5, 0.125, ((0, 16),))
    expert_down = gaussian(streams_of[12], (EXPERTS, EFF, D), EFF ** -0.5, 0.21875, ((0, 16),))
    return dict(queries=queries, keys=keys, values=values, lengths=lengths, owner_counts=owner_counts, row_order=row_order, residual=residual, out_weight=out_weight, norm_gain=norm_gain, expert_ids=expert_ids, route_weights=route_weights, gate_up=gate_up, expert_down=expert_down)


def slot_table(owner_counts, row_order, total_rows, capacity):
    offsets = jnp.cumsum(owner_counts) - owner_counts
    column = jnp.arange(capacity, dtype=jnp.int32)
    where_at = (offsets[:, None] + column[None, :]).astype(jnp.int32)
    filled = column[None, :] < owner_counts[:, None]
    picked = row_order[jnp.clip(where_at, 0, total_rows - 1)]
    return (jnp.where(filled, picked, total_rows).astype(jnp.int32), filled)

def partial_attention(query_rows, key_block, value_block, lengths, first_key):
    requests = lengths.shape[0]
    groups = HQ // KVH
    span = key_block.shape[1]
    query_grid = query_rows.reshape(requests, STRETCH, KVH, groups, HD).astype(jnp.float32)
    key_grid = key_block.reshape(requests, span, KVH, HD).astype(jnp.float32)
    value_grid = value_block.reshape(requests, span, KVH, HD).astype(jnp.float32)

    def one_request(items):
        query_part, key_part, value_part, length = items
        scores = jnp.einsum('cvgh,pvh->vgcp', query_part, key_part, precision=lax.Precision.HIGHEST) * HD ** (-0.5)
        query_pos = length - STRETCH + jnp.arange(STRETCH, dtype=jnp.int32)
        key_pos = first_key + jnp.arange(span, dtype=jnp.int32)
        allowed = key_pos[None, :] <= query_pos[:, None]
        scores = jnp.where(allowed, scores, -1e+30)
        top = lax.optimization_barrier(jnp.max(scores, axis=-1))
        weights = jnp.where(allowed, jnp.exp(scores - top[..., None]), 0.0)
        total = lax.optimization_barrier(jnp.sum(weights, axis=-1))
        rounded = weights.astype(jnp.bfloat16).astype(jnp.float32)
        mixed = jnp.einsum('vgcp,pvh->cvgh', rounded, value_part, precision=lax.Precision.HIGHEST)
        return (mixed.reshape(STRETCH, HQ * HD), jnp.transpose(top, (2, 0, 1)).reshape(STRETCH, HQ), jnp.transpose(total, (2, 0, 1)).reshape(STRETCH, HQ))
    mixed, top, total = lax.map(one_request, (query_grid, key_grid, value_grid, lengths))
    return (mixed.reshape(-1, HQ * HD), top.reshape(-1, HQ), total.reshape(-1, HQ))

def reference(queries, keys, values, lengths, owner_counts, row_order, residual, out_weight, norm_gain, expert_ids, route_weights, gate_up, expert_down):
    key_shards = jnp.moveaxis(keys.reshape(REQS, N_CTX, CACHE_DEV, KVH * HD), 1, 0)
    value_shards = jnp.moveaxis(values.reshape(REQS, N_CTX, CACHE_DEV, KVH * HD), 1, 0)

    def fold(carry, items):
        best, denom, numer = carry
        shard, key_part, value_part = items
        mixed, top, total = partial_attention(queries, key_part, value_part, lengths, (shard * CACHE_DEV).astype(jnp.int32))
        new_best = jnp.maximum(best, top)
        old_factor = jnp.exp(best - new_best)
        new_factor = jnp.exp(top - new_best)
        denom = denom * old_factor + total * new_factor
        numer = (numer.reshape(ROWS, HQ, HD) * old_factor[..., None] + mixed.reshape(ROWS, HQ, HD) * new_factor[..., None]).reshape(ROWS, HQ * HD)
        return ((new_best, denom, numer), None)
    start = (jnp.full((ROWS, HQ), -1e+30, jnp.float32), jnp.zeros((ROWS, HQ), jnp.float32), jnp.zeros((ROWS, HQ * HD), jnp.float32))
    (best, denom, numer), _ = lax.scan(fold, start, (jnp.arange(N_CTX, dtype=jnp.int32), key_shards, value_shards))
    attn = (numer.reshape(ROWS, HQ, HD) / denom[..., None]).reshape(ROWS, HQ * HD).astype(jnp.bfloat16)
    attn_pad = jnp.concatenate([attn, jnp.zeros((1, HQ * HD), jnp.bfloat16)], axis=0)
    slot_rows, filled = slot_table(owner_counts, row_order, ROWS, CAP_ROWS)
    valid = filled.reshape(-1)
    attn_slots = attn_pad[slot_rows.reshape(-1)]
    projected = jnp.dot(attn_slots, out_weight, preferred_element_type=jnp.float32)
    stream = (residual.astype(jnp.float32) + projected).astype(jnp.bfloat16)
    stream_f = stream.astype(jnp.float32)
    normed = (stream_f * lax.rsqrt(lax.optimization_barrier(jnp.mean(stream_f * stream_f, axis=-1, keepdims=True)) + 1e-06) * norm_gain).astype(jnp.bfloat16)
    normed_pad = jnp.concatenate([normed, jnp.zeros((1, D), jnp.bfloat16)], axis=0)
    weight_norm = route_weights / lax.optimization_barrier(jnp.sum(route_weights, axis=-1, keepdims=True))

    def per_expert(moe, items):
        expert, gate_part, down_part = items
        hit = (expert_ids == expert) & valid[:, None]
        chosen = jnp.any(hit, axis=-1)
        weight = lax.optimization_barrier(jnp.sum(jnp.where(hit, weight_norm, 0.0), axis=-1))
        index = jnp.nonzero(chosen, size=N_CTX * ROUTE_CAP, fill_value=SLOTS)[0].astype(jnp.int32)
        rows = normed_pad[index]
        both = jnp.dot(rows, gate_part, preferred_element_type=jnp.float32)
        hidden = (jax.nn.silu(both[:, :EFF]) * both[:, EFF:]).astype(jnp.bfloat16)
        result = jnp.dot(hidden, down_part, preferred_element_type=jnp.float32).astype(jnp.bfloat16)
        weight_pad = jnp.concatenate([weight, jnp.zeros((1,), weight.dtype)])
        moe = moe.at[index].add(weight_pad[index][:, None] * result.astype(jnp.float32))
        return (moe, None)
    moe, _ = lax.scan(per_expert, jnp.zeros((SLOTS + 1, D), jnp.float32), (jnp.arange(EXPERTS, dtype=jnp.int32), gate_up, expert_down))
    layer_out = jnp.where(valid[:, None], stream_f + moe[:SLOTS], 0.0).astype(jnp.bfloat16)
    return (attn_slots, layer_out)
```

```python
import functools

import jax
import jax.numpy as jnp
from jax import lax
from jax.experimental import pallas as pl
from jax.experimental.pallas import tpu as pltpu
from jax.sharding import PartitionSpec as P

D = 2048
HQ = 16
KVH = 2
HD = 128
EFF = 768
TOPK = 8
STRETCH = 128
GROUPS = HQ // KVH
LANES = 128
F32 = jnp.float32
BF16 = jnp.bfloat16
MESH = pl.DeviceIdType.MESH


def dot(a, b, ca, cb):
    return lax.dot_general(a, b, (((ca,), (cb,)), ((), ())), preferred_element_type=F32)


def kernel(
    n,
    lengths,
    counts_ref,
    order_ref,
    q_ref,
    keys_ref,
    values_ref,
    residual_ref,
    ids_ref,
    route_ref,
    gain_ref,
    ow_hbm,
    gu_hbm,
    down_hbm,
    attn_out,
    layer_out,
    ow,
    gu,
    down,
    q_all,
    c_all,
    mix_snd,
    st_snd,
    mix_rcv,
    st_rcv,
    m_snd,
    s_snd,
    m_in,
    s_in,
    a_snd,
    a_in,
    p_snd,
    p_rcv,
    p_mid,
    p_in,
    n_all,
    hid,
    e_snd,
    e_rcv,
    e_mid,
    e_in,
    w_sem,
    q_s,
    q_f,
    q_r,
    c_s,
    c_f,
    c_r,
    pair_s,
    pair_r,
    m_s,
    m_r,
    s_s,
    s_r,
    a_s,
    a_r,
    p_s,
    p_r,
    n_s,
    n_f,
    n_r,
    e_s,
    e_r,
):
    half_n = n // 2
    home = q_ref.shape[0]
    rows = n * home
    cap = residual_ref.shape[0]
    slots = n * cap
    chunk = ow.shape[0]
    span = keys_ref.shape[1]
    requests = keys_ref.shape[0]
    me = lax.axis_index("ctx")
    par = lax.rem(me, 2)
    half = me // 2
    other = 1 - par
    sib = half * 2 + other

    def peer(k):
        return lax.rem(half + k, half_n)

    def remote(src, dst, ss, rs, dev):
        return pltpu.make_async_remote_copy(
            src_ref=src, dst_ref=dst, send_sem=ss, recv_sem=rs,
            device_id={"ctx": dev}, device_id_type=MESH,
        )

    def each(lo, hi, f):
        def step(k, c):
            f(k)
            return c
        lax.fori_loop(lo, hi, step, 0)

    loads = [
        pltpu.make_async_copy(ow_hbm, ow, w_sem.at[0]),
        pltpu.make_async_copy(gu_hbm.at[0], gu, w_sem.at[1]),
        pltpu.make_async_copy(down_hbm.at[0], down, w_sem.at[2]),
    ]

    barrier = pltpu.get_barrier_semaphore()
    each(1, n, lambda k: pl.semaphore_signal(
        barrier, inc=1, device_id={"ctx": lax.rem(me + k, n)}, device_id_type=MESH))

    qf = q_ref[...].astype(F32)
    width = GROUPS * HD
    q_all[par, half] = jnp.concatenate(
        [qf[:, v * width:(v + 1) * width] for v in range(KVH)], axis=0).astype(BF16)

    counts = counts_ref[...].astype(F32)

    def slot_info(index, owner, place):
        lane = lax.broadcasted_iota(jnp.int32, (index, n), 1)
        start = jnp.sum(jnp.where(lane < owner, counts, 0.0), axis=1, keepdims=True)
        held = jnp.sum(jnp.where(lane == owner, counts, 0.0), axis=1, keepdims=True)
        return start, place.astype(F32) < held

    own_place = lax.broadcasted_iota(jnp.int32, (cap, 1), 0)
    _, own_valid = slot_info(cap, jnp.zeros((cap, 1), jnp.int32) + me, own_place)

    ids = ids_ref[...]
    route = route_ref[...]
    route = route / jnp.sum(route, axis=1, keepdims=True)
    expert_lane = lax.broadcasted_iota(jnp.int32, (cap, c_all.shape[-1]), 1)
    mixw = jnp.zeros((cap, c_all.shape[-1]), F32)
    for k in range(TOPK):
        mixw = mixw + jnp.where(expert_lane == ids[:, k:k + 1], route[:, k:k + 1], 0.0)
    c_all[par, half] = jnp.where(own_valid, mixw, 0.0)

    pl.semaphore_wait(barrier, n - 1)

    def gather_start(buf, ss, rs):
        own = buf.at[par, half]
        each(1, half_n, lambda k: remote(
            own, own, ss.at[k], rs.at[par, half], peer(k) * 2 + par).start())
        remote(own, own, ss.at[0], rs.at[par, half], sib).start()

    def gather_forward(buf, ss, fs, rs):
        def step(k):
            q = lax.rem(half - k + half_n, half_n)
            block = buf.at[par, q]
            got = remote(block, block, ss.at[k], rs.at[par, q], sib)
            got.wait_recv()
            remote(block, block, fs.at[k], rs.at[par, q], sib).start()
        each(1, half_n, step)

    def gather_finish(buf, ss, fs, rs):
        def step(q):
            block = buf.at[other, q]
            remote(block, block, ss.at[0], rs.at[other, q], sib).wait_recv()
        each(0, half_n, step)
        own = buf.at[par, half]
        each(0, half_n, lambda k: remote(
            own, own, ss.at[k], rs.at[par, half], sib).wait_send())
        each(1, half_n, lambda k: remote(
            own, own, fs.at[k], rs.at[par, half], sib).wait_send())

    gather_start(q_all, q_s, q_r)
    gather_start(c_all, c_s, c_r)
    for load in loads:
        load.start()

    index = lax.broadcasted_iota(jnp.int32, (slots, 1), 0)
    block_of = index // cap
    owner = lax.rem(block_of, half_n) * 2 + block_of // half_n
    place = lax.rem(index, cap)
    start, filled = slot_info(slots, owner, place)
    at = start + place.astype(F32)
    row_lane = lax.broadcasted_iota(jnp.int32, (slots, rows), 1).astype(F32)
    order = order_ref[...].astype(F32)
    row_of = jnp.sum(jnp.where(row_lane == at, order, 0.0), axis=1, keepdims=True)
    row_of = jnp.where(filled, row_of, -1.0)
    pick = (row_lane == row_of).astype(BF16)

    gather_forward(q_all, q_s, q_f, q_r)
    gather_finish(q_all, q_s, q_f, q_r)

    first_key = me * span
    per_head = HD // chunk
    pair = 2
    for request in range(requests):
        length = lengths[request]
        blocks = STRETCH // home
        lo = request * blocks
        q_req = jnp.stack(
            [q_all[(lo + b) % 2, (lo + b) // 2]
             for b in range(blocks)], axis=0).astype(F32)
        q_req = q_req.reshape(blocks, KVH, home, width)
        key_pos = first_key + lax.broadcasted_iota(jnp.int32, (span, pair * STRETCH), 0)
        row_pos = length - STRETCH + lax.rem(
            lax.broadcasted_iota(jnp.int32, (span, pair * STRETCH), 1), STRETCH)
        allowed = key_pos <= row_pos
        for v in range(KVH):
            key_v = keys_ref[request, :, v * HD:(v + 1) * HD]
            val_v = values_ref[request, :, v * HD:(v + 1) * HD]
            val_t = val_v.astype(F32).T.astype(BF16)
            q_v = q_req[:, v].reshape(STRETCH, width)
            for g in range(0, GROUPS, pair):
                q_g = jnp.concatenate(
                    [q_v[:, (g + i) * HD:(g + i + 1) * HD] for i in range(pair)],
                    axis=0).astype(BF16)
                scores = dot(key_v, q_g, 1, 1) * HD ** (-0.5)
                scores = jnp.where(allowed, scores, -1e30)
                top = jnp.max(scores, axis=0, keepdims=True)
                weights = jnp.where(allowed, jnp.exp(scores - top), 0.0)
                total = jnp.sum(weights, axis=0, keepdims=True)
                mixed = dot(val_t, weights.astype(BF16), 1, 0).astype(BF16)
                for i in range(pair):
                    head = v * GROUPS + g + i
                    cols = slice(request * STRETCH, (request + 1) * STRETCH)
                    take = slice(i * STRETCH, (i + 1) * STRETCH)
                    for c in range(per_head):
                        j = head * per_head + c
                        mix_snd[j % 2, j // 2, :, cols] = mixed[c * chunk:(c + 1) * chunk, take]
                        st_snd[j % 2, 0, j // 2:j // 2 + 1, cols] = top[:, take]
                        st_snd[j % 2, 1, j // 2:j // 2 + 1, cols] = total[:, take]

    x_mix = remote(mix_snd.at[other], mix_rcv, pair_s.at[0], pair_r.at[0], sib)
    x_st = remote(st_snd.at[other], st_rcv, pair_s.at[1], pair_r.at[1], sib)
    x_st.start()
    x_mix.start()
    gather_forward(c_all, c_s, c_f, c_r)
    x_st.wait()
    x_mix.wait()
    top_a, top_b = st_snd[par, 0], st_rcv[0]
    best = jnp.maximum(top_a, top_b)
    fac_a, fac_b = jnp.exp(top_a - best), jnp.exp(top_b - best)
    total = st_snd[par, 1] * fac_a + st_rcv[1] * fac_b
    for q in range(half_n):
        s_snd[q, 0:1] = best[q:q + 1]
        s_snd[q, 1:2] = total[q:q + 1]
        m_snd[q] = (mix_snd[par, q].astype(F32) * fac_a[q:q + 1]
                    + mix_rcv[q].astype(F32) * fac_b[q:q + 1]).astype(BF16)

    def part_copies(k):
        p = peer(k)
        dev = p * 2 + par
        return (
            remote(s_snd.at[p], s_in.at[half], s_s.at[k], s_r.at[half], dev),
            remote(m_snd.at[p], m_in.at[half], m_s.at[k], m_r.at[half], dev),
        )

    def start_parts(k):
        for c in part_copies(k):
            c.start()

    each(1, half_n, start_parts)
    s_in[half, 0:2] = s_snd[half, 0:2]
    m_in[half] = m_snd[half]
    loads[0].wait()

    def wait_parts(k):
        p = peer(k)
        remote(s_snd.at[p], s_in.at[p], s_s.at[k], s_r.at[p], sib).wait_recv()
        remote(m_snd.at[p], m_in.at[p], m_s.at[k], m_r.at[p], sib).wait_recv()

    each(1, half_n, wait_parts)
    best = s_in[0, 0:1]
    for q in range(1, half_n):
        best = jnp.maximum(best, s_in[q, 0:1])
    denom = jnp.zeros_like(best)
    numer = jnp.zeros((chunk, rows), F32)
    for q in range(half_n):
        factor = jnp.exp(s_in[q, 0:1] - best)
        denom = denom + factor * s_in[q, 1:2]
        numer = numer + m_in[q].astype(F32) * factor
    attn = (numer / denom).astype(BF16)

    a_slots = dot(pick, attn, 1, 1).astype(BF16)
    a_snd[...] = a_slots.reshape(2, half_n, cap, chunk)

    def project(parity):
        part = dot(a_snd[parity].reshape(half_n * cap, chunk), ow[...], 1, 0)
        p_snd[parity] = part.astype(BF16).reshape(half_n, cap, D)

    project(other)
    x_p = remote(p_snd.at[other], p_rcv, pair_s.at[2], pair_r.at[2], sib)
    x_p.start()
    project(par)
    x_p.wait()

    def spread(mine, got, mid, into, ss, rs):
        def step(k):
            p = peer(k)
            mid[p] = (mine[par, p].astype(F32) + got[p].astype(F32)).astype(BF16)
            remote(mid.at[p], into.at[half], ss.at[k], rs.at[half], p * 2 + par).start()
        each(1, half_n, step)

    def collect(mine, got, mid, into, ss, rs):
        total = mine[par, half].astype(F32) + got[half].astype(F32)

        def step(k, total):
            p = lax.rem(half - k + half_n, half_n)
            remote(mid.at[p], into.at[p], ss.at[k], rs.at[p], sib).wait_recv()
            return total + into[p].astype(F32)
        return lax.fori_loop(1, half_n, step, total)

    spread(p_snd, p_rcv, p_mid, p_in, p_s, p_r)

    def attn_copy(k):
        to = lax.rem(me + k, n)
        return remote(a_snd.at[lax.rem(to, 2), to // 2], a_in.at[me],
                      a_s.at[k], a_r.at[me], to)

    each(1, n, lambda k: attn_copy(k).start())
    projected = collect(p_snd, p_rcv, p_mid, p_in, p_s, p_r)
    stream = (residual_ref[...].astype(F32) + projected).astype(BF16).astype(F32)
    normed = stream * lax.rsqrt(
        jnp.mean(stream * stream, axis=1, keepdims=True) + 1e-06) * gain_ref[...]
    n_all[par, half] = normed.astype(BF16)
    gather_start(n_all, n_s, n_r)
    gather_finish(c_all, c_s, c_f, c_r)
    loads[1].wait()
    loads[2].wait()
    gather_forward(n_all, n_s, n_f, n_r)
    gather_finish(n_all, n_s, n_f, n_r)

    lane = lax.broadcasted_iota(jnp.int32, (slots // 2, c_all.shape[-1]), 1)
    tile = 256

    def expert(parity):
        x = n_all[parity].reshape(slots // 2, D)

        def up(t, c):
            lo = pl.multiple_of(t * tile, tile)
            gate = dot(x, gu[:, pl.ds(lo, tile)], 1, 0)
            lift = dot(x, gu[:, pl.ds(EFF + lo, tile)], 1, 0)
            hid[:, pl.ds(lo, tile)] = (gate / (1.0 + jnp.exp(-gate)) * lift).astype(BF16)
            return c
        lax.fori_loop(0, EFF // tile, up, 0)
        routes = c_all[parity].reshape(slots // 2, c_all.shape[-1])
        weight = jnp.sum(jnp.where(lane == me, routes, 0.0), axis=1, keepdims=True)
        h = hid[...]

        def lower(t, c):
            lo = pl.multiple_of(t * tile, tile)
            part = dot(h, down[:, pl.ds(lo, tile)], 1, 0) * weight
            e_snd[parity, :, :, pl.ds(lo, tile)] = part.astype(BF16).reshape(
                half_n, cap, tile)
            return c
        lax.fori_loop(0, D // tile, lower, 0)

    expert(other)
    x_e = remote(e_snd.at[other], e_rcv, pair_s.at[3], pair_r.at[3], sib)
    x_e.start()
    expert(par)
    x_e.wait()
    spread(e_snd, e_rcv, e_mid, e_in, e_s, e_r)

    a_in[me] = a_snd[par, half]

    def wait_attn(k):
        at_k = lax.rem(me + k, n)
        remote(a_snd.at[0, 0], a_in.at[at_k], a_s.at[k], a_r.at[at_k], sib).wait_recv()

    each(1, n, wait_attn)
    attn_out[...] = jnp.concatenate([a_in[j] for j in range(n)], axis=1)

    moe = collect(e_snd, e_rcv, e_mid, e_in, e_s, e_r)
    layer_out[...] = jnp.where(own_valid, stream + moe, 0.0).astype(BF16)

    def drain(k):
        for c in part_copies(k):
            c.wait_send()
        remote(p_mid.at[0], p_in.at[0], p_s.at[k], p_r.at[0], sib).wait_send()
        remote(e_mid.at[0], e_in.at[0], e_s.at[k], e_r.at[0], sib).wait_send()

    each(1, half_n, drain)
    each(1, n, lambda k: attn_copy(k).wait_send())


def body(
    queries,
    keys,
    values,
    lengths,
    owner_counts,
    row_order,
    residual,
    out_weight,
    norm_gain,
    expert_ids,
    route_weights,
    gate_up,
    expert_down,
):
    n = lax.axis_size("ctx")
    half_n = n // 2
    home = queries.shape[0]
    rows = n * home
    cap = residual.shape[0]
    chunk = out_weight.shape[0]
    lanes = -(-n // LANES) * LANES
    vmem = pl.BlockSpec(memory_space=pltpu.VMEM)
    smem = pl.BlockSpec(memory_space=pltpu.SMEM)
    anywhere = pl.BlockSpec(memory_space=pl.ANY)
    dma = pltpu.SemaphoreType.DMA
    slot_block = (half_n, cap, D)
    scratch = [
        pltpu.VMEM(out_weight.shape, BF16),
        pltpu.VMEM(gate_up.shape[1:], BF16),
        pltpu.VMEM(expert_down.shape[1:], BF16),
        pltpu.VMEM((2, half_n, KVH * home, GROUPS * HD), BF16),
        pltpu.VMEM((2, half_n, cap, lanes), F32),
        pltpu.VMEM((2, half_n, chunk, rows), BF16),
        pltpu.VMEM((2, 2, half_n, rows), F32),
        pltpu.VMEM((half_n, chunk, rows), BF16),
        pltpu.VMEM((2, half_n, rows), F32),
        pltpu.VMEM((half_n, chunk, rows), BF16),
        pltpu.VMEM((half_n, 8, rows), F32),
        pltpu.VMEM((half_n, chunk, rows), BF16),
        pltpu.VMEM((half_n, 8, rows), F32),
        pltpu.VMEM((2, half_n, cap, chunk), BF16),
        pltpu.VMEM((n, cap, chunk), BF16),
        pltpu.VMEM((2,) + slot_block, BF16),
        pltpu.VMEM(slot_block, BF16),
        pltpu.VMEM(slot_block, BF16),
        pltpu.VMEM(slot_block, BF16),
        pltpu.VMEM((2,) + slot_block, BF16),
        pltpu.VMEM((half_n * cap, EFF), BF16),
        pltpu.VMEM((2,) + slot_block, BF16),
        pltpu.VMEM(slot_block, BF16),
        pltpu.VMEM(slot_block, BF16),
        pltpu.VMEM(slot_block, BF16),
        dma((3,)),
    ]
    gather = [dma((half_n,)), dma((half_n,)), dma((2, half_n))]
    exchange = [dma((half_n,)), dma((half_n,))]
    scratch += gather + gather
    scratch += [dma((4,)), dma((4,))]
    scratch += exchange + exchange
    scratch += [dma((n,)), dma((n,))]
    scratch += exchange + gather + exchange
    return pl.pallas_call(
        functools.partial(kernel, n),
        out_shape=(
            jax.ShapeDtypeStruct((cap, D), BF16),
            jax.ShapeDtypeStruct((cap, D), BF16),
        ),
        in_specs=[smem] + [vmem] * 9 + [anywhere] * 3,
        out_specs=(vmem, vmem),
        scratch_shapes=scratch,
        compiler_params=pltpu.CompilerParams(
            collective_id=0, has_side_effects=True, vmem_limit_bytes=60 * 2**20
        ),
    )(
        lengths,
        owner_counts.reshape(1, n),
        row_order.reshape(1, rows),
        queries,
        keys,
        values,
        residual,
        expert_ids,
        route_weights,
        norm_gain.reshape(1, D),
        out_weight,
        gate_up,
        expert_down,
    )


def solution(mesh):
    placed = (
        P(("groups", "ctx"), None),
        P("groups", "ctx", None),
        P("groups", "ctx", None),
        P("groups"),
        P("groups"),
        P("groups"),
        P(("groups", "ctx"), None),
        P("ctx", None),
        P(),
        P(("groups", "ctx"), None),
        P(("groups", "ctx"), None),
        P("ctx", None, None),
        P("ctx", None, None),
    )
    return jax.shard_map(
        body,
        mesh=mesh,
        in_specs=placed,
        out_specs=(P(("groups", "ctx"), None), P(("groups", "ctx"), None)),
        check_vma=False,
    )
```

```python
import functools

import jax
import jax.numpy as jnp
from jax import lax
from jax.experimental import pallas as pl
from jax.experimental.pallas import tpu as pltpu
from jax.sharding import PartitionSpec as P

D = 2048
HQ = 16
KVH = 2
HD = 128
EFF = 768
TOPK = 8
STRETCH = 128
GROUPS = HQ // KVH
LANES = 128
F32 = jnp.float32
BF16 = jnp.bfloat16
MESH = pl.DeviceIdType.MESH


def dot(a, b, ca, cb):
    return lax.dot_general(a, b, (((ca,), (cb,)), ((), ())), preferred_element_type=F32)


def kernel(
    n,
    lengths,
    counts_ref,
    order_ref,
    q_ref,
    keys_ref,
    values_ref,
    residual_ref,
    ids_ref,
    route_ref,
    gain_ref,
    ow_hbm,
    gu_hbm,
    down_hbm,
    attn_out,
    layer_out,
    ow,
    gu,
    down,
    q_all,
    c_all,
    mix_snd,
    st_snd,
    mix_rcv,
    st_rcv,
    m_snd,
    s_snd,
    m_in,
    s_in,
    a_snd,
    a_in,
    p_snd,
    p_rcv,
    p_mid,
    p_in,
    p_yin,
    n_all,
    hid,
    e_snd,
    e_rcv,
    e_mid,
    e_in,
    e_yin,
    w_sem,
    q_s,
    q_y,
    q_f,
    q_r,
    c_s,
    c_y,
    c_f,
    c_r,
    pair_s,
    pair_r,
    m_s,
    m_r,
    s_s,
    s_r,
    a_s,
    a_r,
    p_s,
    p_y,
    p_r,
    p_yr,
    n_s,
    n_y,
    n_f,
    n_r,
    e_s,
    e_y,
    e_r,
    e_yr,
):
    half_n = n // 2
    home = q_ref.shape[0]
    rows = n * home
    cap = residual_ref.shape[0]
    slots = n * cap
    chunk = ow.shape[0]
    span = keys_ref.shape[1]
    requests = keys_ref.shape[0]
    me = lax.axis_index("ctx")
    par = lax.rem(me, 2)
    half = me // 2
    other = 1 - par
    sib = half * 2 + other

    ny = 2 if half_n % 2 == 0 else 1
    nz = half_n // ny
    z, y = half // ny, lax.rem(half, ny)

    def peer(k):
        return lax.rem(half + k, half_n)

    def remote(src, dst, ss, rs, dev):
        return pltpu.make_async_remote_copy(
            src_ref=src, dst_ref=dst, send_sem=ss, recv_sem=rs,
            device_id={"ctx": dev}, device_id_type=MESH,
        )

    def each(lo, hi, f):
        def step(k, c):
            f(k)
            return c
        lax.fori_loop(lo, hi, step, 0)

    loads = [
        pltpu.make_async_copy(ow_hbm, ow, w_sem.at[0]),
        pltpu.make_async_copy(gu_hbm.at[0], gu, w_sem.at[1]),
        pltpu.make_async_copy(down_hbm.at[0], down, w_sem.at[2]),
    ]

    barrier = pltpu.get_barrier_semaphore()
    each(1, n, lambda k: pl.semaphore_signal(
        barrier, inc=1, device_id={"ctx": lax.rem(me + k, n)}, device_id_type=MESH))

    qf = q_ref[...].astype(F32)
    width = GROUPS * HD
    q_all[par, half] = jnp.concatenate(
        [qf[:, v * width:(v + 1) * width] for v in range(KVH)], axis=0).astype(BF16)

    counts = counts_ref[...].astype(F32)

    def slot_info(index, owner, place):
        lane = lax.broadcasted_iota(jnp.int32, (index, n), 1)
        start = jnp.sum(jnp.where(lane < owner, counts, 0.0), axis=1, keepdims=True)
        held = jnp.sum(jnp.where(lane == owner, counts, 0.0), axis=1, keepdims=True)
        return start, place.astype(F32) < held

    own_place = lax.broadcasted_iota(jnp.int32, (cap, 1), 0)
    _, own_valid = slot_info(cap, jnp.zeros((cap, 1), jnp.int32) + me, own_place)

    def upright(flat):
        return jnp.concatenate([flat, jnp.zeros((TOPK, LANES - cap), F32)], axis=1).T[:cap]

    ids = upright(ids_ref[...].astype(F32)).astype(jnp.int32)
    route = upright(route_ref[...])
    route = route / jnp.sum(route, axis=1, keepdims=True)
    expert_lane = lax.broadcasted_iota(jnp.int32, (cap, c_all.shape[-1]), 1)
    mixw = jnp.zeros((cap, c_all.shape[-1]), F32)
    for k in range(TOPK):
        mixw = mixw + jnp.where(expert_lane == ids[:, k:k + 1], route[:, k:k + 1], 0.0)
    c_all[par, half] = jnp.where(own_valid, mixw, 0.0)

    pl.semaphore_wait(barrier, n - 1)

    def z_peer(k):
        return lax.rem(z + k, nz) * ny + y

    def y_peer(k):
        return lax.rem(z + k, nz) * ny + (ny - 1 - y)

    def block_copy(buf, pa, h, sem, rs, dev):
        block = buf.at[pa, h]
        return remote(block, block, sem, rs.at[pa, h], dev)

    def gather_start(buf, sems):
        ss, ys, fs, rs = sems
        each(1, nz, lambda k: block_copy(
            buf, par, half, ss.at[k], rs, z_peer(k) * 2 + par).start())
        if ny > 1:
            block_copy(buf, par, half, ys.at[0], rs, y_peer(0) * 2 + par).start()
        block_copy(buf, par, half, ss.at[0], rs, sib).start()

    def pass_on(buf, sems, h):
        ss, ys, fs, rs = sems
        block_copy(buf, par, h, ss.at[0], rs, sib).wait_recv()
        block_copy(buf, par, h, fs.at[h], rs, sib).start()

    def gather_z(buf, sems):
        ss, ys, fs, rs = sems
        if ny > 1:
            pass_on(buf, sems, y_peer(0))

        def step(k):
            h = z_peer(nz - k)
            pass_on(buf, sems, h)
            if ny > 1:
                block_copy(buf, par, h, ys.at[k], rs, y_peer(0) * 2 + par).start()
        each(1, nz, step)

    def gather_y(buf, sems):
        if ny > 1:
            each(1, nz, lambda k: pass_on(buf, sems, y_peer(nz - k)))

    def gather_finish(buf, sems):
        ss, ys, fs, rs = sems
        each(0, half_n, lambda h: block_copy(
            buf, other, h, ss.at[0], rs, sib).wait_recv())

    def gather_drain(buf, sems):
        ss, ys, fs, rs = sems
        each(0, nz, lambda k: block_copy(buf, par, half, ss.at[k], rs, sib).wait_send())
        if ny > 1:
            each(0, nz, lambda k: block_copy(buf, par, half, ys.at[k], rs, sib).wait_send())
        each(1, half_n, lambda k: block_copy(
            buf, par, peer(k), fs.at[peer(k)], rs, sib).wait_send())

    q_g = (q_s, q_y, q_f, q_r)
    c_g = (c_s, c_y, c_f, c_r)
    n_g = (n_s, n_y, n_f, n_r)
    gather_start(q_all, q_g)
    for load in loads:
        load.start()

    index = lax.broadcasted_iota(jnp.int32, (slots, 1), 0)
    block_of = index // cap
    owner = lax.rem(block_of, half_n) * 2 + block_of // half_n
    place = lax.rem(index, cap)
    start, filled = slot_info(slots, owner, place)
    at = start + place.astype(F32)
    row_lane = lax.broadcasted_iota(jnp.int32, (slots, rows), 1).astype(F32)
    order = order_ref[...].astype(F32)
    row_of = jnp.sum(jnp.where(row_lane == at, order, 0.0), axis=1, keepdims=True)
    row_of = jnp.where(filled, row_of, -1.0)
    pick = (row_lane == row_of).astype(BF16)

    gather_z(q_all, q_g)
    gather_y(q_all, q_g)
    gather_finish(q_all, q_g)
    gather_start(c_all, c_g)

    first_key = me * span
    per_head = HD // chunk
    pair = 2
    for request in range(requests):
        length = lengths[request]
        blocks = STRETCH // home
        lo = request * blocks
        q_req = jnp.stack(
            [q_all[(lo + b) % 2, (lo + b) // 2]
             for b in range(blocks)], axis=0).astype(F32)
        q_req = q_req.reshape(blocks, KVH, home, width)
        key_pos = first_key + lax.broadcasted_iota(jnp.int32, (span, pair * STRETCH), 0)
        row_pos = length - STRETCH + lax.rem(
            lax.broadcasted_iota(jnp.int32, (span, pair * STRETCH), 1), STRETCH)
        allowed = key_pos <= row_pos
        for v in range(KVH):
            key_v = keys_ref[request, :, v * HD:(v + 1) * HD]
            val_v = values_ref[request, :, v * HD:(v + 1) * HD]
            val_t = val_v.astype(F32).T.astype(BF16)
            q_v = q_req[:, v].reshape(STRETCH, width)
            for g in range(0, GROUPS, pair):
                q_pair = jnp.concatenate(
                    [q_v[:, (g + i) * HD:(g + i + 1) * HD] for i in range(pair)],
                    axis=0).astype(BF16)
                scores = dot(key_v, q_pair, 1, 1) * HD ** (-0.5)
                scores = jnp.where(allowed, scores, -1e30)
                top = jnp.max(scores, axis=0, keepdims=True)
                weights = jnp.where(allowed, jnp.exp(scores - top), 0.0)
                total = jnp.sum(weights, axis=0, keepdims=True)
                mixed = dot(val_t, weights.astype(BF16), 1, 0).astype(BF16)
                for i in range(pair):
                    head = v * GROUPS + g + i
                    cols = slice(request * STRETCH, (request + 1) * STRETCH)
                    take = slice(i * STRETCH, (i + 1) * STRETCH)
                    for c in range(per_head):
                        j = head * per_head + c
                        mix_snd[j % 2, j // 2, :, cols] = mixed[c * chunk:(c + 1) * chunk, take]
                        st_snd[j % 2, 0, j // 2:j // 2 + 1, cols] = top[:, take]
                        st_snd[j % 2, 1, j // 2:j // 2 + 1, cols] = total[:, take]

    x_mix = remote(mix_snd.at[other], mix_rcv, pair_s.at[0], pair_r.at[0], sib)
    x_st = remote(st_snd.at[other], st_rcv, pair_s.at[1], pair_r.at[1], sib)
    x_st.start()
    x_mix.start()
    gather_z(c_all, c_g)
    x_st.wait()
    x_mix.wait()
    top_a, top_b = st_snd[par, 0], st_rcv[0]
    best = jnp.maximum(top_a, top_b)
    fac_a, fac_b = jnp.exp(top_a - best), jnp.exp(top_b - best)
    total = st_snd[par, 1] * fac_a + st_rcv[1] * fac_b
    for q in range(half_n):
        s_snd[q, 0:1] = best[q:q + 1]
        s_snd[q, 1:2] = total[q:q + 1]
        m_snd[q] = (mix_snd[par, q].astype(F32) * fac_a[q:q + 1]
                    + mix_rcv[q].astype(F32) * fac_b[q:q + 1]).astype(BF16)

    def part_copies(k):
        p = peer(k)
        dev = p * 2 + par
        return (
            remote(s_snd.at[p], s_in.at[half], s_s.at[k], s_r.at[half], dev),
            remote(m_snd.at[p], m_in.at[half], m_s.at[k], m_r.at[half], dev),
        )

    def start_parts(k):
        for c in part_copies(k):
            c.start()

    each(1, half_n, start_parts)
    gather_y(c_all, c_g)
    s_in[half, 0:2] = s_snd[half, 0:2]
    m_in[half] = m_snd[half]
    loads[0].wait()

    def wait_parts(k):
        p = peer(k)
        remote(s_snd.at[p], s_in.at[p], s_s.at[k], s_r.at[p], sib).wait_recv()
        remote(m_snd.at[p], m_in.at[p], m_s.at[k], m_r.at[p], sib).wait_recv()

    each(1, half_n, wait_parts)
    best = s_in[0, 0:1]
    for q in range(1, half_n):
        best = jnp.maximum(best, s_in[q, 0:1])
    denom = jnp.zeros_like(best)
    numer = jnp.zeros((chunk, rows), F32)
    for q in range(half_n):
        factor = jnp.exp(s_in[q, 0:1] - best)
        denom = denom + factor * s_in[q, 1:2]
        numer = numer + m_in[q].astype(F32) * factor
    attn = (numer / denom).astype(BF16)

    a_slots = dot(pick, attn, 1, 1).astype(BF16)
    a_snd[...] = a_slots.reshape(2, half_n, cap, chunk)

    def project(parity):
        part = dot(a_snd[parity].reshape(half_n * cap, chunk), ow[...], 1, 0)
        p_snd[parity] = part.astype(BF16).reshape(half_n, cap, D)

    project(other)
    x_p = remote(p_snd.at[other], p_rcv, pair_s.at[2], pair_r.at[2], sib)
    x_p.start()
    project(par)
    x_p.wait()

    def spread(mine, got, mid, into, yin, ss, ys, rs, yr):
        if ny > 1:
            def step_y(k):
                h = y_peer(k)
                to = h // ny
                mid[h] = (mine[par, h].astype(F32) + got[h].astype(F32)).astype(BF16)
                remote(mid.at[h], yin.at[to], ys.at[k - 1], yr.at[to],
                       y_peer(0) * 2 + par).start()
            each(1, nz + 1, step_y)

        def step(k):
            h = z_peer(k)
            total = mine[par, h].astype(F32) + got[h].astype(F32)
            if ny > 1:
                to = h // ny
                remote(mid.at[h], yin.at[to], ss.at[k], yr.at[to], sib).wait_recv()
                total = total + yin[to].astype(F32)
            mid[h] = total.astype(BF16)
            remote(mid.at[h], into.at[z], ss.at[k], rs.at[z], h * 2 + par).start()
        each(1, nz, step)

    def collect(mine, got, mid, into, yin, ss, ys, rs, yr):
        total = mine[par, half].astype(F32) + got[half].astype(F32)
        if ny > 1:
            remote(mid.at[0], yin.at[z], ss.at[0], yr.at[z], sib).wait_recv()
            total = total + yin[z].astype(F32)

        def step(k, total):
            at_z = lax.rem(z - k + nz, nz)
            remote(mid.at[0], into.at[at_z], ss.at[k], rs.at[at_z], sib).wait_recv()
            return total + into[at_z].astype(F32)
        return lax.fori_loop(1, nz, step, total)

    def drain_spread(mid, into, yin, ss, ys, rs, yr):
        each(1, nz, lambda k: remote(
            mid.at[0], into.at[0], ss.at[k], rs.at[0], sib).wait_send())
        if ny > 1:
            each(0, nz, lambda k: remote(
                mid.at[0], yin.at[0], ys.at[k], yr.at[0], sib).wait_send())

    p_x = (p_mid, p_in, p_yin, p_s, p_y, p_r, p_yr)
    e_x = (e_mid, e_in, e_yin, e_s, e_y, e_r, e_yr)
    spread(p_snd, p_rcv, *p_x)

    def attn_copy(k):
        to = lax.rem(me + k, n)
        return remote(a_snd.at[lax.rem(to, 2), to // 2], a_in.at[me],
                      a_s.at[k], a_r.at[me], to)

    each(1, n, lambda k: attn_copy(k).start())
    projected = collect(p_snd, p_rcv, *p_x)
    stream = (residual_ref[...].astype(F32) + projected).astype(BF16).astype(F32)
    normed = stream * lax.rsqrt(
        jnp.mean(stream * stream, axis=1, keepdims=True) + 1e-06) * gain_ref[...]
    n_all[par, half] = normed.astype(BF16)
    gather_start(n_all, n_g)
    gather_finish(c_all, c_g)
    loads[1].wait()
    loads[2].wait()
    gather_z(n_all, n_g)
    gather_y(n_all, n_g)
    gather_finish(n_all, n_g)

    lane = lax.broadcasted_iota(jnp.int32, (slots // 2, c_all.shape[-1]), 1)
    tile = 256

    def expert(parity):
        x = n_all[parity].reshape(slots // 2, D)

        def up(t, c):
            lo = pl.multiple_of(t * tile, tile)
            gate = dot(x, gu[:, pl.ds(lo, tile)], 1, 0)
            lift = dot(x, gu[:, pl.ds(EFF + lo, tile)], 1, 0)
            hid[:, pl.ds(lo, tile)] = (gate / (1.0 + jnp.exp(-gate)) * lift).astype(BF16)
            return c
        lax.fori_loop(0, EFF // tile, up, 0)
        routes = c_all[parity].reshape(slots // 2, c_all.shape[-1])
        weight = jnp.sum(jnp.where(lane == me, routes, 0.0), axis=1, keepdims=True)
        h = hid[...]

        def lower(t, c):
            lo = pl.multiple_of(t * tile, tile)
            part = dot(h, down[:, pl.ds(lo, tile)], 1, 0) * weight
            e_snd[parity, :, :, pl.ds(lo, tile)] = part.astype(BF16).reshape(
                half_n, cap, tile)
            return c
        lax.fori_loop(0, D // tile, lower, 0)

    expert(other)
    x_e = remote(e_snd.at[other], e_rcv, pair_s.at[3], pair_r.at[3], sib)
    x_e.start()
    expert(par)
    x_e.wait()
    spread(e_snd, e_rcv, *e_x)

    a_in[me] = a_snd[par, half]

    def wait_attn(k):
        at_k = lax.rem(me + k, n)
        remote(a_snd.at[0, 0], a_in.at[at_k], a_s.at[k], a_r.at[at_k], sib).wait_recv()

    each(1, n, wait_attn)
    attn_out[...] = jnp.concatenate([a_in[j] for j in range(n)], axis=1)

    moe = collect(e_snd, e_rcv, *e_x)
    layer_out[...] = jnp.where(own_valid, stream + moe, 0.0).astype(BF16)

    def drain(k):
        for c in part_copies(k):
            c.wait_send()

    each(1, half_n, drain)
    drain_spread(*p_x)
    drain_spread(*e_x)
    gather_drain(q_all, q_g)
    gather_drain(c_all, c_g)
    gather_drain(n_all, n_g)
    each(1, n, lambda k: attn_copy(k).wait_send())


def body(
    queries,
    keys,
    values,
    lengths,
    owner_counts,
    row_order,
    residual,
    out_weight,
    norm_gain,
    expert_ids,
    route_weights,
    gate_up,
    expert_down,
):
    n = lax.axis_size("ctx")
    half_n = n // 2
    home = queries.shape[0]
    rows = n * home
    cap = residual.shape[0]
    chunk = out_weight.shape[0]
    lanes = -(-n // LANES) * LANES
    vmem = pl.BlockSpec(memory_space=pltpu.VMEM)
    smem = pl.BlockSpec(memory_space=pltpu.SMEM)
    anywhere = pl.BlockSpec(memory_space=pl.ANY)
    dma = pltpu.SemaphoreType.DMA
    slot_block = (half_n, cap, D)
    ny = 2 if half_n % 2 == 0 else 1
    nz = half_n // ny
    line_block = (nz, cap, D)
    scratch = [
        pltpu.VMEM(out_weight.shape, BF16),
        pltpu.VMEM(gate_up.shape[1:], BF16),
        pltpu.VMEM(expert_down.shape[1:], BF16),
        pltpu.VMEM((2, half_n, KVH * home, GROUPS * HD), BF16),
        pltpu.VMEM((2, half_n, cap, lanes), F32),
        pltpu.VMEM((2, half_n, chunk, rows), BF16),
        pltpu.VMEM((2, 2, half_n, rows), F32),
        pltpu.VMEM((half_n, chunk, rows), BF16),
        pltpu.VMEM((2, half_n, rows), F32),
        pltpu.VMEM((half_n, chunk, rows), BF16),
        pltpu.VMEM((half_n, 8, rows), F32),
        pltpu.VMEM((half_n, chunk, rows), BF16),
        pltpu.VMEM((half_n, 8, rows), F32),
        pltpu.VMEM((2, half_n, cap, chunk), BF16),
        pltpu.VMEM((n, cap, chunk), BF16),
        pltpu.VMEM((2,) + slot_block, BF16),
        pltpu.VMEM(slot_block, BF16),
        pltpu.VMEM(slot_block, BF16),
        pltpu.VMEM(line_block, BF16),
        pltpu.VMEM(line_block, BF16),
        pltpu.VMEM((2,) + slot_block, BF16),
        pltpu.VMEM((half_n * cap, EFF), BF16),
        pltpu.VMEM((2,) + slot_block, BF16),
        pltpu.VMEM(slot_block, BF16),
        pltpu.VMEM(slot_block, BF16),
        pltpu.VMEM(line_block, BF16),
        pltpu.VMEM(line_block, BF16),
        dma((3,)),
    ]
    gather = [dma((nz,)), dma((nz,)), dma((half_n,)), dma((2, half_n))]
    exchange = [dma((half_n,)), dma((half_n,))]
    staged = [dma((nz,)), dma((nz,)), dma((nz,)), dma((nz,))]
    scratch += gather + gather
    scratch += [dma((4,)), dma((4,))]
    scratch += exchange + exchange
    scratch += [dma((n,)), dma((n,))]
    scratch += staged + gather + staged
    return pl.pallas_call(
        functools.partial(kernel, n),
        out_shape=(
            jax.ShapeDtypeStruct((cap, D), BF16),
            jax.ShapeDtypeStruct((cap, D), BF16),
        ),
        in_specs=[smem] + [vmem] * 9 + [anywhere] * 3,
        out_specs=(vmem, vmem),
        scratch_shapes=scratch,
        compiler_params=pltpu.CompilerParams(
            collective_id=0, has_side_effects=True, vmem_limit_bytes=60 * 2**20
        ),
    )(
        lengths,
        owner_counts.reshape(1, n),
        row_order.reshape(1, rows),
        queries,
        keys,
        values,
        residual,
        expert_ids.T,
        route_weights.T,
        norm_gain.reshape(1, D),
        out_weight,
        gate_up,
        expert_down,
    )


def solution(mesh):
    placed = (
        P(("groups", "ctx"), None),
        P("groups", "ctx", None),
        P("groups", "ctx", None),
        P("groups"),
        P("groups"),
        P("groups"),
        P(("groups", "ctx"), None),
        P("ctx", None),
        P(),
        P(("groups", "ctx"), None),
        P(("groups", "ctx"), None),
        P("ctx", None, None),
        P("ctx", None, None),
    )
    return jax.shard_map(
        body,
        mesh=mesh,
        in_specs=placed,
        out_specs=(P(("groups", "ctx"), None), P(("groups", "ctx"), None)),
        check_vma=False,
    )
```

```python
import functools

import jax
import jax.numpy as jnp
from jax import lax
from jax.experimental import pallas as pl
from jax.experimental.pallas import tpu as pltpu
from jax.sharding import PartitionSpec as P

D = 2048
HQ = 16
KVH = 2
HD = 128
EFF = 768
TOPK = 8
STRETCH = 128
GROUPS = HQ // KVH
LANES = 128
LOG2E = 1.4426950408889634
F32 = jnp.float32
BF16 = jnp.bfloat16
MESH = pl.DeviceIdType.MESH


def dot(a, b, ca, cb):
    return lax.dot_general(a, b, (((ca,), (cb,)), ((), ())), preferred_element_type=F32)


def kernel(
    n,
    lengths,
    counts_ref,
    order_ref,
    q_ref,
    keys_hbm,
    values_hbm,
    residual_hbm,
    ids_ref,
    route_ref,
    gain_ref,
    ow_hbm,
    gu_hbm,
    down_hbm,
    out,
    keys_ref,
    values_ref,
    residual_ref,
    ow,
    gu,
    down,
    q_all,
    c_all,
    mix_snd,
    st_snd,
    mix_rcv,
    st_rcv,
    m_snd,
    s_snd,
    m_in,
    s_in,
    a_snd,
    a_in,
    p_snd,
    p_rcv,
    p_mid,
    p_in,
    p_yin,
    n_all,
    hid,
    e_snd,
    e_rcv,
    e_mid,
    e_in,
    e_yin,
    w_sem,
    q_s,
    q_y,
    q_f,
    q_r,
    c_s,
    c_y,
    c_f,
    c_r,
    pair_s,
    pair_r,
    m_s,
    m_r,
    s_s,
    s_r,
    a_s,
    a_r,
    p_s,
    p_y,
    p_r,
    p_yr,
    n_s,
    n_y,
    n_f,
    n_r,
    e_s,
    e_y,
    e_r,
    e_yr,
):
    half_n = n // 2
    home = q_ref.shape[0]
    rows = n * home
    cap = residual_ref.shape[0]
    slots = n * cap
    chunk = ow.shape[0]
    span = keys_ref.shape[1]
    requests = keys_ref.shape[0]
    me = lax.axis_index("ctx")
    par = lax.rem(me, 2)
    half = me // 2
    other = 1 - par
    sib = half * 2 + other

    ny = 2 if half_n % 2 == 0 else 1
    nz = half_n // ny
    z, y = half // ny, lax.rem(half, ny)

    def peer(k):
        return lax.rem(half + k, half_n)

    def remote(src, dst, ss, rs, dev):
        return pltpu.make_async_remote_copy(
            src_ref=src, dst_ref=dst, send_sem=ss, recv_sem=rs,
            device_id={"ctx": dev}, device_id_type=MESH,
        )

    def each(lo, hi, f):
        def step(k, c):
            f(k)
            return c
        lax.fori_loop(lo, hi, step, 0)

    loads = [
        pltpu.make_async_copy(ow_hbm, ow, w_sem.at[0]),
        pltpu.make_async_copy(gu_hbm.at[0], gu, w_sem.at[1]),
        pltpu.make_async_copy(down_hbm.at[0], down, w_sem.at[2]),
        pltpu.make_async_copy(residual_hbm, residual_ref, w_sem.at[5]),
    ]

    cache = [
        pltpu.make_async_copy(keys_hbm, keys_ref, w_sem.at[3]),
        pltpu.make_async_copy(values_hbm, values_ref, w_sem.at[4]),
    ]
    for load in cache:
        load.start()

    barrier = pltpu.get_barrier_semaphore()
    each(1, n, lambda k: pl.semaphore_signal(
        barrier, inc=1, device_id={"ctx": lax.rem(me + k, n)}, device_id_type=MESH))

    qf = q_ref[...].astype(F32)
    width = GROUPS * HD
    q_all[par, half] = jnp.concatenate(
        [qf[:, v * width:(v + 1) * width] for v in range(KVH)], axis=0).astype(BF16)

    counts = counts_ref[...].astype(F32)

    def slot_info(index, owner, place):
        lane = lax.broadcasted_iota(jnp.int32, (index, n), 1)
        start = jnp.sum(jnp.where(lane < owner, counts, 0.0), axis=1, keepdims=True)
        held = jnp.sum(jnp.where(lane == owner, counts, 0.0), axis=1, keepdims=True)
        return start, place.astype(F32) < held

    own_place = lax.broadcasted_iota(jnp.int32, (cap, 1), 0)
    _, own_valid = slot_info(cap, jnp.zeros((cap, 1), jnp.int32) + me, own_place)

    def upright(flat):
        return jnp.concatenate([flat, jnp.zeros((TOPK, LANES - cap), F32)], axis=1).T[:cap]

    ids = upright(ids_ref[...].astype(F32)).astype(jnp.int32)
    route = upright(route_ref[...])
    route = route / jnp.sum(route, axis=1, keepdims=True)
    expert_lane = lax.broadcasted_iota(jnp.int32, (cap, c_all.shape[-1]), 1)
    mixw = jnp.zeros((cap, c_all.shape[-1]), F32)
    for k in range(TOPK):
        mixw = mixw + jnp.where(expert_lane == ids[:, k:k + 1], route[:, k:k + 1], 0.0)
    c_all[par, half] = jnp.where(own_valid, mixw, 0.0)

    pl.semaphore_wait(barrier, n - 1)

    def z_peer(k):
        return lax.rem(z + k, nz) * ny + y

    def y_peer(k):
        return lax.rem(z + k, nz) * ny + (ny - 1 - y)

    def block_copy(buf, pa, h, sem, rs, dev):
        block = buf.at[pa, h]
        return remote(block, block, sem, rs.at[pa, h], dev)

    def gather_start(buf, sems):
        ss, ys, fs, rs = sems
        each(1, nz, lambda k: block_copy(
            buf, par, half, ss.at[k], rs, z_peer(k) * 2 + par).start())
        if ny > 1:
            block_copy(buf, par, half, ys.at[0], rs, y_peer(0) * 2 + par).start()
        block_copy(buf, par, half, ss.at[0], rs, sib).start()

    def pass_on(buf, sems, h):
        ss, ys, fs, rs = sems
        block_copy(buf, par, h, ss.at[0], rs, sib).wait_recv()
        block_copy(buf, par, h, fs.at[h], rs, sib).start()

    def gather_z(buf, sems):
        ss, ys, fs, rs = sems
        if ny > 1:
            pass_on(buf, sems, y_peer(0))

        def step(k):
            h = z_peer(nz - k)
            pass_on(buf, sems, h)
            if ny > 1:
                block_copy(buf, par, h, ys.at[k], rs, y_peer(0) * 2 + par).start()
        each(1, nz, step)

    def gather_y(buf, sems):
        if ny > 1:
            each(1, nz, lambda k: pass_on(buf, sems, y_peer(nz - k)))

    def gather_finish(buf, sems):
        ss, ys, fs, rs = sems
        each(0, half_n, lambda h: block_copy(
            buf, other, h, ss.at[0], rs, sib).wait_recv())

    def gather_drain(buf, sems):
        ss, ys, fs, rs = sems
        each(0, nz, lambda k: block_copy(buf, par, half, ss.at[k], rs, sib).wait_send())
        if ny > 1:
            each(0, nz, lambda k: block_copy(buf, par, half, ys.at[k], rs, sib).wait_send())
        each(1, half_n, lambda k: block_copy(
            buf, par, peer(k), fs.at[peer(k)], rs, sib).wait_send())

    q_g = (q_s, q_y, q_f, q_r)
    c_g = (c_s, c_y, c_f, c_r)
    n_g = (n_s, n_y, n_f, n_r)
    gather_start(q_all, q_g)
    for load in loads:
        load.start()

    index = lax.broadcasted_iota(jnp.int32, (slots, 1), 0)
    block_of = index // cap
    owner = lax.rem(block_of, half_n) * 2 + block_of // half_n
    place = lax.rem(index, cap)
    start, filled = slot_info(slots, owner, place)
    at = start + place.astype(F32)
    row_lane = lax.broadcasted_iota(jnp.int32, (slots, rows), 1).astype(F32)
    order = order_ref[...].astype(F32)
    row_of = jnp.sum(jnp.where(row_lane == at, order, 0.0), axis=1, keepdims=True)
    row_of = jnp.where(filled, row_of, -1.0)
    pick = (row_lane == row_of).astype(BF16)

    gather_z(q_all, q_g)
    gather_y(q_all, q_g)
    gather_finish(q_all, q_g)
    gather_start(c_all, c_g)
    for load in cache:
        load.wait()

    first_key = me * span
    per_head = HD // chunk
    pair = 2
    for request in range(requests):
        length = lengths[request]
        blocks = STRETCH // home
        lo = request * blocks
        q_req = jnp.stack(
            [q_all[(lo + b) % 2, (lo + b) // 2]
             for b in range(blocks)], axis=0).astype(F32)
        q_req = q_req.reshape(blocks, KVH, home, width)
        key_pos = first_key + lax.broadcasted_iota(jnp.int32, (span, pair * STRETCH), 0)
        row_pos = length - STRETCH + lax.rem(
            lax.broadcasted_iota(jnp.int32, (span, pair * STRETCH), 1), STRETCH)
        allowed = key_pos <= row_pos
        for v in range(KVH):
            key_v = keys_ref[request, :, v * HD:(v + 1) * HD]
            val_v = values_ref[request, :, v * HD:(v + 1) * HD]
            val_t = val_v.astype(F32).T.astype(BF16)
            q_v = q_req[:, v].reshape(STRETCH, width)
            for g in range(0, GROUPS, pair):
                q_pair = jnp.concatenate(
                    [q_v[:, (g + i) * HD:(g + i + 1) * HD] for i in range(pair)],
                    axis=0).astype(BF16)
                scores = jnp.where(allowed, dot(key_v, q_pair, 1, 1), -1e30)
                top = jnp.max(scores, axis=0, keepdims=True)
                some = top > -1e29
                weights = jnp.exp2((scores - top) * (HD ** (-0.5) * LOG2E))
                total = jnp.where(some, jnp.sum(weights, axis=0, keepdims=True), 0.0)
                mixed = dot(val_t, weights.astype(BF16), 1, 0)
                mixed = jnp.where(some, mixed, 0.0).astype(BF16)
                top = jnp.where(some, top * HD ** (-0.5), -1e30)
                for i in range(pair):
                    head = v * GROUPS + g + i
                    cols = slice(request * STRETCH, (request + 1) * STRETCH)
                    take = slice(i * STRETCH, (i + 1) * STRETCH)
                    for c in range(per_head):
                        j = head * per_head + c
                        mix_snd[j % 2, j // 2, :, cols] = mixed[c * chunk:(c + 1) * chunk, take]
                        st_snd[j % 2, 0, j // 2:j // 2 + 1, cols] = top[:, take]
                        st_snd[j % 2, 1, j // 2:j // 2 + 1, cols] = total[:, take]

    x_mix = remote(mix_snd.at[other], mix_rcv, pair_s.at[0], pair_r.at[0], sib)
    x_st = remote(st_snd.at[other], st_rcv, pair_s.at[1], pair_r.at[1], sib)
    x_st.start()
    x_mix.start()
    gather_z(c_all, c_g)
    x_st.wait()
    x_mix.wait()
    top_a, top_b = st_snd[par, 0], st_rcv[0]
    best = jnp.maximum(top_a, top_b)
    fac_a, fac_b = jnp.exp(top_a - best), jnp.exp(top_b - best)
    total = st_snd[par, 1] * fac_a + st_rcv[1] * fac_b
    for q in range(half_n):
        s_snd[q, 0:1] = best[q:q + 1]
        s_snd[q, 1:2] = total[q:q + 1]
        m_snd[q] = (mix_snd[par, q].astype(F32) * fac_a[q:q + 1]
                    + mix_rcv[q].astype(F32) * fac_b[q:q + 1]).astype(BF16)

    def part_copies(k):
        p = peer(k)
        dev = p * 2 + par
        return (
            remote(s_snd.at[p], s_in.at[half], s_s.at[k], s_r.at[half], dev),
            remote(m_snd.at[p], m_in.at[half], m_s.at[k], m_r.at[half], dev),
        )

    def start_parts(k):
        for c in part_copies(k):
            c.start()

    each(1, half_n, start_parts)
    gather_y(c_all, c_g)
    s_in[half, 0:2] = s_snd[half, 0:2]
    m_in[half] = m_snd[half]
    loads[0].wait()
    loads[3].wait()

    def wait_parts(k):
        p = peer(k)
        remote(s_snd.at[p], s_in.at[p], s_s.at[k], s_r.at[p], sib).wait_recv()
        remote(m_snd.at[p], m_in.at[p], m_s.at[k], m_r.at[p], sib).wait_recv()

    each(1, half_n, wait_parts)
    best = s_in[0, 0:1]
    for q in range(1, half_n):
        best = jnp.maximum(best, s_in[q, 0:1])
    denom = jnp.zeros_like(best)
    numer = jnp.zeros((chunk, rows), F32)
    for q in range(half_n):
        factor = jnp.exp(s_in[q, 0:1] - best)
        denom = denom + factor * s_in[q, 1:2]
        numer = numer + m_in[q].astype(F32) * factor
    attn = (numer / denom).astype(BF16)

    a_slots = dot(pick, attn, 1, 1).astype(BF16)
    a_snd[...] = a_slots.reshape(2, half_n, cap, chunk)

    def project(parity):
        part = dot(a_snd[parity].reshape(half_n * cap, chunk), ow[...], 1, 0)
        p_snd[parity] = part.astype(BF16).reshape(half_n, cap, D)

    def attn_copy(k):
        to = lax.rem(me + k, n)
        return remote(a_snd.at[lax.rem(to, 2), to // 2], a_in.at[me],
                      a_s.at[k], a_r.at[me], to)

    each(1, n, lambda k: attn_copy(k).start())
    project(other)
    x_p = remote(p_snd.at[other], p_rcv, pair_s.at[2], pair_r.at[2], sib)
    x_p.start()
    project(par)
    x_p.wait()

    def spread(mine, got, mid, into, yin, ss, ys, rs, yr):
        if ny > 1:
            def step_y(k):
                h = y_peer(k)
                to = h // ny
                mid[h] = (mine[par, h].astype(F32) + got[h].astype(F32)).astype(BF16)
                remote(mid.at[h], yin.at[to], ys.at[k - 1], yr.at[to],
                       y_peer(0) * 2 + par).start()
            each(1, nz + 1, step_y)

        def step(k):
            h = z_peer(k)
            total = mine[par, h].astype(F32) + got[h].astype(F32)
            if ny > 1:
                to = h // ny
                remote(mid.at[h], yin.at[to], ss.at[k], yr.at[to], sib).wait_recv()
                total = total + yin[to].astype(F32)
            mid[h] = total.astype(BF16)
            remote(mid.at[h], into.at[z], ss.at[k], rs.at[z], h * 2 + par).start()
        each(1, nz, step)

    def collect(mine, got, mid, into, yin, ss, ys, rs, yr):
        total = mine[par, half].astype(F32) + got[half].astype(F32)
        if ny > 1:
            remote(mid.at[0], yin.at[z], ss.at[0], yr.at[z], sib).wait_recv()
            total = total + yin[z].astype(F32)

        def step(k, total):
            at_z = lax.rem(z - k + nz, nz)
            remote(mid.at[0], into.at[at_z], ss.at[k], rs.at[at_z], sib).wait_recv()
            return total + into[at_z].astype(F32)
        return lax.fori_loop(1, nz, step, total)

    def drain_spread(mid, into, yin, ss, ys, rs, yr):
        each(1, nz, lambda k: remote(
            mid.at[0], into.at[0], ss.at[k], rs.at[0], sib).wait_send())
        if ny > 1:
            each(0, nz, lambda k: remote(
                mid.at[0], yin.at[0], ys.at[k], yr.at[0], sib).wait_send())

    p_x = (p_mid, p_in, p_yin, p_s, p_y, p_r, p_yr)
    e_x = (e_mid, e_in, e_yin, e_s, e_y, e_r, e_yr)
    spread(p_snd, p_rcv, *p_x)

    projected = collect(p_snd, p_rcv, *p_x)
    stream = (residual_ref[...].astype(F32) + projected).astype(BF16).astype(F32)
    normed = stream * lax.rsqrt(
        jnp.mean(stream * stream, axis=1, keepdims=True) + 1e-06) * gain_ref[...]
    n_all[par, half] = normed.astype(BF16)
    gather_start(n_all, n_g)
    gather_finish(c_all, c_g)
    loads[1].wait()
    loads[2].wait()
    gather_z(n_all, n_g)
    gather_y(n_all, n_g)
    gather_finish(n_all, n_g)

    lane = lax.broadcasted_iota(jnp.int32, (slots, c_all.shape[-1]), 1)
    tile = 256
    x = n_all.reshape(slots, D)

    def up(t, c):
        lo = pl.multiple_of(t * tile, tile)
        gate = dot(x[...], gu[:, pl.ds(lo, tile)], 1, 0)
        lift = dot(x[...], gu[:, pl.ds(EFF + lo, tile)], 1, 0)
        hid[:, pl.ds(lo, tile)] = (gate / (1.0 + jnp.exp(-gate)) * lift).astype(BF16)
        return c
    lax.fori_loop(0, EFF // tile, up, 0)
    routes = c_all[...].reshape(slots, c_all.shape[-1])
    weight = jnp.sum(jnp.where(lane == me, routes, 0.0), axis=1, keepdims=True)

    def lower(t, c):
        lo = pl.multiple_of(t * tile, tile)
        part = dot(hid[...], down[:, pl.ds(lo, tile)], 1, 0) * weight
        e_snd[:, :, :, pl.ds(lo, tile)] = part.astype(BF16).reshape(2, half_n, cap, tile)
        return c

    sides = []
    side = D // 2
    for i in range(2):
        lax.fori_loop(i * side // tile, (i + 1) * side // tile, lower, 0)
        cols = pl.ds(i * side, side)
        sides.append(remote(
            e_snd.at[other, :, :, cols], e_rcv.at[:, :, cols],
            pair_s.at[3 + i], pair_r.at[3 + i], sib))
        sides[i].start()
    for x_e in sides:
        x_e.wait()
    spread(e_snd, e_rcv, *e_x)

    a_in[me] = a_snd[par, half]

    def wait_attn(k):
        at_k = lax.rem(me + k, n)
        remote(a_snd.at[0, 0], a_in.at[at_k], a_s.at[k], a_r.at[at_k], sib).wait_recv()

    each(1, n, wait_attn)
    out[0] = jnp.concatenate([a_in[j] for j in range(n)], axis=1)

    moe = collect(e_snd, e_rcv, *e_x)
    out[1] = jnp.where(own_valid, stream + moe, 0.0).astype(BF16)

    def drain(k):
        for c in part_copies(k):
            c.wait_send()

    each(1, half_n, drain)
    drain_spread(*p_x)
    drain_spread(*e_x)
    gather_drain(q_all, q_g)
    gather_drain(c_all, c_g)
    gather_drain(n_all, n_g)
    each(1, n, lambda k: attn_copy(k).wait_send())


def body(
    queries,
    keys,
    values,
    lengths,
    owner_counts,
    row_order,
    residual,
    out_weight,
    norm_gain,
    expert_ids,
    route_weights,
    gate_up,
    expert_down,
):
    n = lax.axis_size("ctx")
    half_n = n // 2
    home = queries.shape[0]
    rows = n * home
    cap = residual.shape[0]
    chunk = out_weight.shape[0]
    lanes = -(-n // LANES) * LANES
    vmem = pl.BlockSpec(memory_space=pltpu.VMEM)
    smem = pl.BlockSpec(memory_space=pltpu.SMEM)
    anywhere = pl.BlockSpec(memory_space=pl.ANY)
    dma = pltpu.SemaphoreType.DMA
    slot_block = (half_n, cap, D)
    ny = 2 if half_n % 2 == 0 else 1
    nz = half_n // ny
    line_block = (nz, cap, D)
    scratch = [
        pltpu.VMEM(keys.shape, BF16),
        pltpu.VMEM(values.shape, BF16),
        pltpu.VMEM(residual.shape, BF16),
        pltpu.VMEM(out_weight.shape, BF16),
        pltpu.VMEM(gate_up.shape[1:], BF16),
        pltpu.VMEM(expert_down.shape[1:], BF16),
        pltpu.VMEM((2, half_n, KVH * home, GROUPS * HD), BF16),
        pltpu.VMEM((2, half_n, cap, lanes), F32),
        pltpu.VMEM((2, half_n, chunk, rows), BF16),
        pltpu.VMEM((2, 2, half_n, rows), F32),
        pltpu.VMEM((half_n, chunk, rows), BF16),
        pltpu.VMEM((2, half_n, rows), F32),
        pltpu.VMEM((half_n, chunk, rows), BF16),
        pltpu.VMEM((half_n, 8, rows), F32),
        pltpu.VMEM((half_n, chunk, rows), BF16),
        pltpu.VMEM((half_n, 8, rows), F32),
        pltpu.VMEM((2, half_n, cap, chunk), BF16),
        pltpu.VMEM((n, cap, chunk), BF16),
        pltpu.VMEM((2,) + slot_block, BF16),
        pltpu.VMEM(slot_block, BF16),
        pltpu.VMEM(slot_block, BF16),
        pltpu.VMEM(line_block, BF16),
        pltpu.VMEM(line_block, BF16),
        pltpu.VMEM((2,) + slot_block, BF16),
        pltpu.VMEM((n * cap, EFF), BF16),
        pltpu.VMEM((2,) + slot_block, BF16),
        pltpu.VMEM(slot_block, BF16),
        pltpu.VMEM(slot_block, BF16),
        pltpu.VMEM(line_block, BF16),
        pltpu.VMEM(line_block, BF16),
        dma((6,)),
    ]
    gather = [dma((nz,)), dma((nz,)), dma((half_n,)), dma((2, half_n))]
    exchange = [dma((half_n,)), dma((half_n,))]
    staged = [dma((nz,)), dma((nz,)), dma((nz,)), dma((nz,))]
    scratch += gather + gather
    scratch += [dma((5,)), dma((5,))]
    scratch += exchange + exchange
    scratch += [dma((n,)), dma((n,))]
    scratch += staged + gather + staged
    out = pl.pallas_call(
        functools.partial(kernel, n),
        out_shape=jax.ShapeDtypeStruct((2, cap, D), BF16),
        in_specs=[smem] + [vmem] * 3 + [anywhere] * 3 + [vmem] * 3 + [anywhere] * 3,
        out_specs=vmem,
        scratch_shapes=scratch,
        compiler_params=pltpu.CompilerParams(
            collective_id=0, has_side_effects=True, vmem_limit_bytes=60 * 2**20
        ),
    )(
        lengths,
        owner_counts.reshape(1, n),
        row_order.reshape(1, rows),
        queries,
        keys,
        values,
        residual,
        expert_ids.T,
        route_weights.T,
        norm_gain.reshape(1, D),
        out_weight,
        gate_up,
        expert_down,
    )
    return out[0], out[1]


def solution(mesh):
    placed = (
        P(("groups", "ctx"), None),
        P("groups", "ctx", None),
        P("groups", "ctx", None),
        P("groups"),
        P("groups"),
        P("groups"),
        P(("groups", "ctx"), None),
        P("ctx", None),
        P(),
        P(("groups", "ctx"), None),
        P(("groups", "ctx"), None),
        P("ctx", None, None),
        P("ctx", None, None),
    )
    return jax.shard_map(
        body,
        mesh=mesh,
        in_specs=placed,
        out_specs=(P(("groups", "ctx"), None), P(("groups", "ctx"), None)),
        check_vma=False,
    )
```

```python
import functools

import jax
import jax.numpy as jnp
from jax import lax
from jax.experimental import pallas as pl
from jax.experimental.pallas import tpu as pltpu
from jax.sharding import PartitionSpec as P

D = 2048
HQ = 16
KVH = 2
HD = 128
EFF = 768
TOPK = 8
STRETCH = 128
GROUPS = HQ // KVH
LANES = 128
LOG2E = 1.4426950408889634
F32 = jnp.float32
BF16 = jnp.bfloat16
MESH = pl.DeviceIdType.MESH


def dot(a, b, ca, cb):
    return lax.dot_general(a, b, (((ca,), (cb,)), ((), ())), preferred_element_type=F32)


def kernel(
    n,
    lengths,
    counts_ref,
    order_ref,
    q_ref,
    keys_hbm,
    values_hbm,
    residual_hbm,
    ids_ref,
    route_ref,
    gain_ref,
    ow_hbm,
    gu_hbm,
    down_hbm,
    out,
    keys_ref,
    values_ref,
    ow,
    gu,
    down,
    q_all,
    c_all,
    mix_snd,
    st_snd,
    mix_rcv,
    st_rcv,
    m_snd,
    s_snd,
    m_in,
    s_in,
    a_snd,
    a_in,
    p_snd,
    p_rcv,
    p_mid,
    p_in,
    p_yin,
    r_all,
    n_all,
    x_buf,
    str_buf,
    hid,
    e_snd,
    e_rcv,
    e_mid,
    e_in,
    e_yin,
    w_sem,
    q_s,
    q_y,
    q_f,
    q_r,
    c_s,
    c_y,
    c_f,
    c_r,
    pair_s,
    pair_r,
    m_s,
    m_r,
    s_s,
    s_r,
    a_s,
    a_r,
    p_s,
    p_y,
    p_r,
    p_yr,
    r_s,
    r_y,
    r_f,
    r_r,
    n_s,
    n_y,
    n_f,
    n_r,
    e_s,
    e_y,
    e_r,
    e_yr,
):
    half_n = n // 2
    home = q_ref.shape[0]
    rows = n * home
    cap = residual_hbm.shape[0]
    slots = n * cap
    chunk = ow.shape[0]
    span = keys_ref.shape[1]
    requests = keys_ref.shape[0]
    me = lax.axis_index("ctx")
    par = lax.rem(me, 2)
    half = me // 2
    other = 1 - par
    sib = half * 2 + other

    ny = 2 if half_n % 2 == 0 else 1
    nz = half_n // ny
    z, y = half // ny, lax.rem(half, ny)

    def peer(k):
        return lax.rem(half + k, half_n)

    def remote(src, dst, ss, rs, dev):
        return pltpu.make_async_remote_copy(
            src_ref=src, dst_ref=dst, send_sem=ss, recv_sem=rs,
            device_id={"ctx": dev}, device_id_type=MESH,
        )

    def each(lo, hi, f):
        def step(k, c):
            f(k)
            return c
        lax.fori_loop(lo, hi, step, 0)

    loads = [
        pltpu.make_async_copy(ow_hbm, ow, w_sem.at[0]),
        pltpu.make_async_copy(gu_hbm.at[0], gu, w_sem.at[1]),
        pltpu.make_async_copy(down_hbm.at[0], down, w_sem.at[2]),
    ]

    cache = [
        pltpu.make_async_copy(keys_hbm, keys_ref, w_sem.at[3]),
        pltpu.make_async_copy(values_hbm, values_ref, w_sem.at[4]),
    ]
    load_res = pltpu.make_async_copy(residual_hbm, r_all.at[par, half], w_sem.at[5])
    load_res.start()
    for load in cache:
        load.start()

    barrier = pltpu.get_barrier_semaphore()
    each(1, n, lambda k: pl.semaphore_signal(
        barrier, inc=1, device_id={"ctx": lax.rem(me + k, n)}, device_id_type=MESH))

    qf = q_ref[...].astype(F32)
    width = GROUPS * HD
    q_all[par, half] = jnp.concatenate(
        [qf[:, v * width:(v + 1) * width] for v in range(KVH)], axis=0).astype(BF16)

    counts = counts_ref[...].astype(F32)

    def slot_info(index, owner, place):
        lane = lax.broadcasted_iota(jnp.int32, (index, n), 1)
        start = jnp.sum(jnp.where(lane < owner, counts, 0.0), axis=1, keepdims=True)
        held = jnp.sum(jnp.where(lane == owner, counts, 0.0), axis=1, keepdims=True)
        return start, place.astype(F32) < held

    own_place = lax.broadcasted_iota(jnp.int32, (cap, 1), 0)
    _, own_valid = slot_info(cap, jnp.zeros((cap, 1), jnp.int32) + me, own_place)

    def upright(flat):
        return jnp.concatenate([flat, jnp.zeros((TOPK, LANES - cap), F32)], axis=1).T[:cap]

    ids = upright(ids_ref[...].astype(F32)).astype(jnp.int32)
    route = upright(route_ref[...])
    route = route / jnp.sum(route, axis=1, keepdims=True)
    expert_lane = lax.broadcasted_iota(jnp.int32, (cap, c_all.shape[-1]), 1)
    mixw = jnp.zeros((cap, c_all.shape[-1]), F32)
    for k in range(TOPK):
        mixw = mixw + jnp.where(expert_lane == ids[:, k:k + 1], route[:, k:k + 1], 0.0)
    c_all[par, half] = jnp.where(own_valid, mixw, 0.0)

    pl.semaphore_wait(barrier, n - 1)

    def z_peer(k):
        return lax.rem(z + k, nz) * ny + y

    def y_peer(k):
        return lax.rem(z + k, nz) * ny + (ny - 1 - y)

    def block_copy(buf, pa, h, sem, rs, dev):
        block = buf.at[pa, h]
        return remote(block, block, sem, rs.at[pa, h], dev)

    def gather_start(buf, sems):
        ss, ys, fs, rs = sems
        each(1, nz, lambda k: block_copy(
            buf, par, half, ss.at[k], rs, z_peer(k) * 2 + par).start())
        if ny > 1:
            block_copy(buf, par, half, ys.at[0], rs, y_peer(0) * 2 + par).start()
        block_copy(buf, par, half, ss.at[0], rs, sib).start()

    def pass_on(buf, sems, h):
        ss, ys, fs, rs = sems
        block_copy(buf, par, h, ss.at[0], rs, sib).wait_recv()
        block_copy(buf, par, h, fs.at[h], rs, sib).start()

    def gather_z(buf, sems):
        ss, ys, fs, rs = sems
        if ny > 1:
            pass_on(buf, sems, y_peer(0))

        def step(k):
            h = z_peer(nz - k)
            pass_on(buf, sems, h)
            if ny > 1:
                block_copy(buf, par, h, ys.at[k], rs, y_peer(0) * 2 + par).start()
        each(1, nz, step)

    def gather_y(buf, sems):
        if ny > 1:
            each(1, nz, lambda k: pass_on(buf, sems, y_peer(nz - k)))

    def gather_finish(buf, sems):
        ss, ys, fs, rs = sems
        each(0, half_n, lambda h: block_copy(
            buf, other, h, ss.at[0], rs, sib).wait_recv())

    def gather_drain(buf, sems):
        ss, ys, fs, rs = sems
        each(0, nz, lambda k: block_copy(buf, par, half, ss.at[k], rs, sib).wait_send())
        if ny > 1:
            each(0, nz, lambda k: block_copy(buf, par, half, ys.at[k], rs, sib).wait_send())
        each(1, half_n, lambda k: block_copy(
            buf, par, peer(k), fs.at[peer(k)], rs, sib).wait_send())

    q_g = (q_s, q_y, q_f, q_r)
    c_g = (c_s, c_y, c_f, c_r)
    r_g = (r_s, r_y, r_f, r_r)
    n_g = (n_s, n_y, n_f, n_r)
    gather_start(q_all, q_g)
    for load in loads:
        load.start()

    index = lax.broadcasted_iota(jnp.int32, (slots, 1), 0)
    block_of = index // cap
    owner = lax.rem(block_of, half_n) * 2 + block_of // half_n
    place = lax.rem(index, cap)
    start, filled = slot_info(slots, owner, place)
    at = start + place.astype(F32)
    row_lane = lax.broadcasted_iota(jnp.int32, (slots, rows), 1).astype(F32)
    order = order_ref[...].astype(F32)
    row_of = jnp.sum(jnp.where(row_lane == at, order, 0.0), axis=1, keepdims=True)
    row_of = jnp.where(filled, row_of, -1.0)
    pick = (row_lane == row_of).astype(BF16)
    lane = lax.broadcasted_iota(jnp.int32, (slots, rows), 1)
    block_lane = lane // home
    device_lane = lax.rem(block_lane, half_n) * 2 + block_lane // half_n
    row_lane = (device_lane * home + lax.rem(lane, home)).astype(F32)
    pick_par = (row_lane == row_of).astype(BF16)
    own_lane = me * home + lax.broadcasted_iota(jnp.int32, (slots, LANES), 1)
    pick_own = (own_lane.astype(F32) == row_of).astype(BF16)

    gather_z(q_all, q_g)
    gather_y(q_all, q_g)
    gather_finish(q_all, q_g)
    gather_start(c_all, c_g)
    load_res.wait()
    gather_start(r_all, r_g)
    for load in cache:
        load.wait()

    first_key = me * span
    per_head = HD // chunk
    pair = 2
    for request in range(requests):
        length = lengths[request]
        blocks = STRETCH // home
        lo = request * blocks
        q_req = jnp.stack(
            [q_all[(lo + b) % 2, (lo + b) // 2]
             for b in range(blocks)], axis=0).astype(F32)
        q_req = q_req.reshape(blocks, KVH, home, width)
        key_pos = first_key + lax.broadcasted_iota(jnp.int32, (span, pair * STRETCH), 0)
        row_pos = length - STRETCH + lax.rem(
            lax.broadcasted_iota(jnp.int32, (span, pair * STRETCH), 1), STRETCH)
        allowed = key_pos <= row_pos
        for v in range(KVH):
            key_v = keys_ref[request, :, v * HD:(v + 1) * HD]
            val_v = values_ref[request, :, v * HD:(v + 1) * HD]
            val_t = val_v.astype(F32).T.astype(BF16)
            q_v = q_req[:, v].reshape(STRETCH, width)
            for g in range(0, GROUPS, pair):
                q_pair = jnp.concatenate(
                    [q_v[:, (g + i) * HD:(g + i + 1) * HD] for i in range(pair)],
                    axis=0).astype(BF16)
                scores = jnp.where(allowed, dot(key_v, q_pair, 1, 1), -1e30)
                top = jnp.max(scores, axis=0, keepdims=True)
                some = top > -1e29
                weights = jnp.exp2((scores - top) * (HD ** (-0.5) * LOG2E))
                total = jnp.where(some, jnp.sum(weights, axis=0, keepdims=True), 0.0)
                mixed = dot(val_t, weights.astype(BF16), 1, 0)
                mixed = jnp.where(some, mixed, 0.0).astype(BF16)
                top = jnp.where(some, top * HD ** (-0.5), -1e30)
                for i in range(pair):
                    head = v * GROUPS + g + i
                    cols = slice(request * STRETCH, (request + 1) * STRETCH)
                    take = slice(i * STRETCH, (i + 1) * STRETCH)
                    for c in range(per_head):
                        j = head * per_head + c
                        mix_snd[j % 2, j // 2, :, cols] = mixed[c * chunk:(c + 1) * chunk, take]
                        st_snd[j % 2, 0, j // 2:j // 2 + 1, cols] = top[:, take]
                        st_snd[j % 2, 1, j // 2:j // 2 + 1, cols] = total[:, take]

    x_mix = remote(mix_snd.at[other], mix_rcv, pair_s.at[0], pair_r.at[0], sib)
    x_st = remote(st_snd.at[other], st_rcv, pair_s.at[1], pair_r.at[1], sib)
    x_st.start()
    x_mix.start()
    gather_z(c_all, c_g)
    x_st.wait()
    x_mix.wait()
    top_a, top_b = st_snd[par, 0], st_rcv[0]
    best = jnp.maximum(top_a, top_b)
    fac_a, fac_b = jnp.exp(top_a - best), jnp.exp(top_b - best)
    total = st_snd[par, 1] * fac_a + st_rcv[1] * fac_b
    for q in range(half_n):
        s_snd[q, 0:1] = best[q:q + 1]
        s_snd[q, 1:2] = total[q:q + 1]
        m_snd[q] = (mix_snd[par, q].astype(F32) * fac_a[q:q + 1]
                    + mix_rcv[q].astype(F32) * fac_b[q:q + 1]).astype(BF16)

    def part_copies(k):
        p = peer(k)
        dev = p * 2 + par
        return (
            remote(s_snd.at[p], s_in.at[half], s_s.at[k], s_r.at[half], dev),
            remote(m_snd.at[p], m_in.at[half], m_s.at[k], m_r.at[half], dev),
        )

    def start_parts(k):
        for c in part_copies(k):
            c.start()

    each(1, half_n, start_parts)
    gather_y(c_all, c_g)
    gather_z(r_all, r_g)
    s_in[half, 0:2] = s_snd[half, 0:2]
    m_in[half] = m_snd[half]
    loads[0].wait()

    def wait_parts(k):
        p = peer(k)
        remote(s_snd.at[p], s_in.at[p], s_s.at[k], s_r.at[p], sib).wait_recv()
        remote(m_snd.at[p], m_in.at[p], m_s.at[k], m_r.at[p], sib).wait_recv()

    each(1, half_n, wait_parts)
    best = s_in[0, 0:1]
    for q in range(1, half_n):
        best = jnp.maximum(best, s_in[q, 0:1])
    denom = jnp.zeros_like(best)
    numer = jnp.zeros((chunk, rows), F32)
    for q in range(half_n):
        factor = jnp.exp(s_in[q, 0:1] - best)
        denom = denom + factor * s_in[q, 1:2]
        numer = numer + m_in[q].astype(F32) * factor
    attn = (numer / denom).astype(BF16)

    a_slots = dot(pick, attn, 1, 1).astype(BF16)
    a_snd[...] = a_slots.reshape(2, half_n, cap, chunk)

    def attn_copy(k):
        to = lax.rem(me + k, n)
        return remote(a_snd.at[lax.rem(to, 2), to // 2], a_in.at[me],
                      a_s.at[k], a_r.at[me], to)

    each(1, n, lambda k: attn_copy(k).start())
    part = dot(attn, ow[...], 0, 0)
    wide = D // 2
    for d in range(n):
        own = part[d * home:(d + 1) * home]
        p_snd[d % 2, d // 2] = jnp.concatenate(
            [own[:, :wide], own[:, wide:]], axis=0).astype(BF16)
    x_p = remote(p_snd.at[other], p_rcv, pair_s.at[2], pair_r.at[2], sib)
    x_p.start()
    gather_y(r_all, r_g)
    x_p.wait()

    def spread(mine, got, mid, into, yin, ss, ys, rs, yr):
        if ny > 1:
            def step_y(k):
                h = y_peer(k)
                to = h // ny
                mid[h] = (mine[par, h].astype(F32) + got[h].astype(F32)).astype(BF16)
                remote(mid.at[h], yin.at[to], ys.at[k - 1], yr.at[to],
                       y_peer(0) * 2 + par).start()
            each(1, nz + 1, step_y)

        def step(k):
            h = z_peer(k)
            total = mine[par, h].astype(F32) + got[h].astype(F32)
            if ny > 1:
                to = h // ny
                remote(mid.at[h], yin.at[to], ss.at[k], yr.at[to], sib).wait_recv()
                total = total + yin[to].astype(F32)
            mid[h] = total.astype(BF16)
            remote(mid.at[h], into.at[z], ss.at[k], rs.at[z], h * 2 + par).start()
        each(1, nz, step)

    def collect(mine, got, mid, into, yin, ss, ys, rs, yr):
        total = mine[par, half].astype(F32) + got[half].astype(F32)
        if ny > 1:
            remote(mid.at[0], yin.at[z], ss.at[0], yr.at[z], sib).wait_recv()
            total = total + yin[z].astype(F32)

        def step(k, total):
            at_z = lax.rem(z - k + nz, nz)
            remote(mid.at[0], into.at[at_z], ss.at[k], rs.at[at_z], sib).wait_recv()
            return total + into[at_z].astype(F32)
        return lax.fori_loop(1, nz, step, total)

    def drain_spread(mid, into, yin, ss, ys, rs, yr):
        each(1, nz, lambda k: remote(
            mid.at[0], into.at[0], ss.at[k], rs.at[0], sib).wait_send())
        if ny > 1:
            each(0, nz, lambda k: remote(
                mid.at[0], yin.at[0], ys.at[k], yr.at[0], sib).wait_send())

    p_x = (p_mid, p_in, p_yin, p_s, p_y, p_r, p_yr)
    e_x = (e_mid, e_in, e_yin, e_s, e_y, e_r, e_yr)
    spread(p_snd, p_rcv, *p_x)

    gather_finish(r_all, r_g)
    held = dot(pick_own, r_all[...].reshape(slots, D), 0, 0)[:home]
    held = jnp.concatenate([held[:, :wide], held[:, wide:]], axis=0)
    projected = collect(p_snd, p_rcv, *p_x)
    stream = (held + projected).astype(BF16).astype(F32)
    square = jnp.sum(stream * stream, axis=1, keepdims=True)
    scale = lax.rsqrt((square[:home] + square[home:]) / D + 1e-06)
    gain = gain_ref[...]
    gain = jnp.concatenate(
        [jnp.broadcast_to(gain[:, :wide], (home, wide)),
         jnp.broadcast_to(gain[:, wide:], (home, wide))], axis=0)
    normed = stream * jnp.concatenate([scale, scale], axis=0) * gain
    n_all[par, half] = normed.astype(BF16)
    gather_start(n_all, n_g)
    blank = jnp.zeros((LANES - home, D), F32)
    str_buf[...] = jnp.concatenate(
        [jnp.concatenate([stream[:home], stream[home:]], axis=1), blank], axis=0).astype(BF16)
    gather_finish(c_all, c_g)
    loads[1].wait()
    loads[2].wait()
    gather_z(n_all, n_g)
    gather_y(n_all, n_g)
    gather_finish(n_all, n_g)

    lane = lax.broadcasted_iota(jnp.int32, (slots, c_all.shape[-1]), 1)
    tile = 256
    halves = n_all[...].astype(F32).reshape(n, 2, home, wide)
    x_buf[:, :wide] = halves[:, 0].reshape(rows, wide).astype(BF16)
    x_buf[:, wide:] = halves[:, 1].reshape(rows, wide).astype(BF16)

    def up(t, c):
        lo = pl.multiple_of(t * tile, tile)
        gate = dot(x_buf[...], gu[:, pl.ds(lo, tile)], 1, 0)
        lift = dot(x_buf[...], gu[:, pl.ds(EFF + lo, tile)], 1, 0)
        hid[:, pl.ds(lo, tile)] = (gate / (1.0 + jnp.exp(-gate)) * lift).astype(BF16)
        return c
    lax.fori_loop(0, EFF // tile, up, 0)
    routes = c_all[...].reshape(slots, c_all.shape[-1])
    weight = jnp.sum(jnp.where(lane == me, routes, 0.0), axis=1, keepdims=True)

    def lower(t, c):
        lo = pl.multiple_of(t * tile, tile)
        result = dot(hid[...], down[:, pl.ds(lo, tile)], 1, 0).astype(BF16)
        part = dot(pick_par, result, 1, 0) * weight
        part = part + dot(pick_own, str_buf[:, pl.ds(lo, tile)], 1, 0)
        e_snd[:, :, :, pl.ds(lo, tile)] = part.astype(BF16).reshape(2, half_n, cap, tile)
        return c

    sides = []
    side = D // 2
    for i in range(2):
        lax.fori_loop(i * side // tile, (i + 1) * side // tile, lower, 0)
        cols = pl.ds(i * side, side)
        sides.append(remote(
            e_snd.at[other, :, :, cols], e_rcv.at[:, :, cols],
            pair_s.at[3 + i], pair_r.at[3 + i], sib))
        sides[i].start()
    for x_e in sides:
        x_e.wait()
    spread(e_snd, e_rcv, *e_x)

    a_in[me] = a_snd[par, half]

    def wait_attn(k):
        at_k = lax.rem(me + k, n)
        remote(a_snd.at[0, 0], a_in.at[at_k], a_s.at[k], a_r.at[at_k], sib).wait_recv()

    each(1, n, wait_attn)
    out[0] = jnp.concatenate([a_in[j] for j in range(n)], axis=1)

    moe = collect(e_snd, e_rcv, *e_x)
    out[1] = jnp.where(own_valid, moe, 0.0).astype(BF16)

    def drain(k):
        for c in part_copies(k):
            c.wait_send()

    each(1, half_n, drain)
    drain_spread(*p_x)
    drain_spread(*e_x)
    gather_drain(q_all, q_g)
    gather_drain(c_all, c_g)
    gather_drain(r_all, r_g)
    gather_drain(n_all, n_g)
    each(1, n, lambda k: attn_copy(k).wait_send())


def body(
    queries,
    keys,
    values,
    lengths,
    owner_counts,
    row_order,
    residual,
    out_weight,
    norm_gain,
    expert_ids,
    route_weights,
    gate_up,
    expert_down,
):
    n = lax.axis_size("ctx")
    half_n = n // 2
    home = queries.shape[0]
    rows = n * home
    cap = residual.shape[0]
    chunk = out_weight.shape[0]
    lanes = -(-n // LANES) * LANES
    vmem = pl.BlockSpec(memory_space=pltpu.VMEM)
    smem = pl.BlockSpec(memory_space=pltpu.SMEM)
    anywhere = pl.BlockSpec(memory_space=pl.ANY)
    dma = pltpu.SemaphoreType.DMA
    slot_block = (half_n, cap, D)
    ny = 2 if half_n % 2 == 0 else 1
    nz = half_n // ny
    line_block = (nz, cap, D)
    row_block = (half_n, 2 * home, D // 2)
    scratch = [
        pltpu.VMEM(keys.shape, BF16),
        pltpu.VMEM(values.shape, BF16),
        pltpu.VMEM(out_weight.shape, BF16),
        pltpu.VMEM(gate_up.shape[1:], BF16),
        pltpu.VMEM(expert_down.shape[1:], BF16),
        pltpu.VMEM((2, half_n, KVH * home, GROUPS * HD), BF16),
        pltpu.VMEM((2, half_n, cap, lanes), F32),
        pltpu.VMEM((2, half_n, chunk, rows), BF16),
        pltpu.VMEM((2, 2, half_n, rows), F32),
        pltpu.VMEM((half_n, chunk, rows), BF16),
        pltpu.VMEM((2, half_n, rows), F32),
        pltpu.VMEM((half_n, chunk, rows), BF16),
        pltpu.VMEM((half_n, 8, rows), F32),
        pltpu.VMEM((half_n, chunk, rows), BF16),
        pltpu.VMEM((half_n, 8, rows), F32),
        pltpu.VMEM((2, half_n, cap, chunk), BF16),
        pltpu.VMEM((n, cap, chunk), BF16),
        pltpu.VMEM((2,) + row_block, BF16),
        pltpu.VMEM(row_block, BF16),
        pltpu.VMEM(row_block, BF16),
        pltpu.VMEM((nz,) + row_block[1:], BF16),
        pltpu.VMEM((nz,) + row_block[1:], BF16),
        pltpu.VMEM((2,) + slot_block, BF16),
        pltpu.VMEM((2,) + row_block, BF16),
        pltpu.VMEM((rows, D), BF16),
        pltpu.VMEM((LANES, D), BF16),
        pltpu.VMEM((rows, EFF), BF16),
        pltpu.VMEM((2,) + slot_block, BF16),
        pltpu.VMEM(slot_block, BF16),
        pltpu.VMEM(slot_block, BF16),
        pltpu.VMEM(line_block, BF16),
        pltpu.VMEM(line_block, BF16),
        dma((6,)),
    ]
    gather = [dma((nz,)), dma((nz,)), dma((half_n,)), dma((2, half_n))]
    exchange = [dma((half_n,)), dma((half_n,))]
    staged = [dma((nz,)), dma((nz,)), dma((nz,)), dma((nz,))]
    scratch += gather + gather
    scratch += [dma((5,)), dma((5,))]
    scratch += exchange + exchange
    scratch += [dma((n,)), dma((n,))]
    scratch += staged + gather + gather + staged
    out = pl.pallas_call(
        functools.partial(kernel, n),
        out_shape=jax.ShapeDtypeStruct((2, cap, D), BF16),
        in_specs=[smem] + [vmem] * 3 + [anywhere] * 3 + [vmem] * 3 + [anywhere] * 3,
        out_specs=vmem,
        scratch_shapes=scratch,
        compiler_params=pltpu.CompilerParams(
            collective_id=0, has_side_effects=True, vmem_limit_bytes=60 * 2**20
        ),
    )(
        lengths,
        owner_counts.reshape(1, n),
        row_order.reshape(1, rows),
        queries,
        keys,
        values,
        residual,
        expert_ids.T,
        route_weights.T,
        norm_gain.reshape(1, D),
        out_weight,
        gate_up,
        expert_down,
    )
    return out[0], out[1]


def solution(mesh):
    placed = (
        P(("groups", "ctx"), None),
        P("groups", "ctx", None),
        P("groups", "ctx", None),
        P("groups"),
        P("groups"),
        P("groups"),
        P(("groups", "ctx"), None),
        P("ctx", None),
        P(),
        P(("groups", "ctx"), None),
        P(("groups", "ctx"), None),
        P("ctx", None, None),
        P("ctx", None, None),
    )
    return jax.shard_map(
        body,
        mesh=mesh,
        in_specs=placed,
        out_specs=(P(("groups", "ctx"), None), P(("groups", "ctx"), None)),
        check_vma=False,
    )
```

```python
import functools

import jax
import jax.numpy as jnp
from jax import lax
from jax.experimental import pallas as pl
from jax.experimental.pallas import tpu as pltpu
from jax.sharding import PartitionSpec as P

D = 2048
HQ = 16
KVH = 2
HD = 128
EFF = 768
TOPK = 8
STRETCH = 128
GROUPS = HQ // KVH
LANES = 128
LOG2E = 1.4426950408889634
F32 = jnp.float32
BF16 = jnp.bfloat16
MESH = pl.DeviceIdType.MESH


def dot(a, b, ca, cb):
    return lax.dot_general(a, b, (((ca,), (cb,)), ((), ())), preferred_element_type=F32)


def kernel(
    n,
    lengths,
    counts_ref,
    order_ref,
    q_ref,
    keys_hbm,
    values_hbm,
    residual_hbm,
    ids_ref,
    route_ref,
    gain_ref,
    ow_hbm,
    gu_hbm,
    down_hbm,
    out,
    keys_ref,
    values_ref,
    ow,
    gu,
    down,
    q_all,
    c_all,
    mix_snd,
    st_snd,
    mix_rcv,
    st_rcv,
    m_snd,
    s_snd,
    m_in,
    s_in,
    a_snd,
    a_in,
    p_snd,
    p_rcv,
    p_mid,
    p_in,
    p_yin,
    r_all,
    n_all,
    x_buf,
    str_buf,
    hid,
    e_snd,
    e_rcv,
    e_mid,
    e_in,
    e_yin,
    w_sem,
    q_s,
    q_y,
    q_f,
    q_r,
    c_s,
    c_y,
    c_f,
    c_r,
    pair_s,
    pair_r,
    m_s,
    m_r,
    s_s,
    s_r,
    a_s,
    a_r,
    p_s,
    p_y,
    p_r,
    p_yr,
    r_s,
    r_y,
    r_f,
    r_r,
    n_s,
    n_y,
    n_f,
    n_r,
    e_s,
    e_y,
    e_r,
    e_yr,
):
    half_n = n // 2
    home = q_ref.shape[0]
    rows = n * home
    cap = residual_hbm.shape[0]
    slots = n * cap
    chunk = ow.shape[0]
    span = keys_ref.shape[1]
    requests = keys_ref.shape[0]
    me = lax.axis_index("ctx")
    par = lax.rem(me, 2)
    half = me // 2
    other = 1 - par
    sib = half * 2 + other

    ny = 2 if half_n % 2 == 0 else 1
    nz = half_n // ny
    z, y = half // ny, lax.rem(half, ny)

    def peer(k):
        return lax.rem(half + k, half_n)

    def remote(src, dst, ss, rs, dev):
        return pltpu.make_async_remote_copy(
            src_ref=src, dst_ref=dst, send_sem=ss, recv_sem=rs,
            device_id={"ctx": dev}, device_id_type=MESH,
        )

    def each(lo, hi, f):
        def step(k, c):
            f(k)
            return c
        lax.fori_loop(lo, hi, step, 0)

    loads = [
        pltpu.make_async_copy(ow_hbm, ow, w_sem.at[0]),
        pltpu.make_async_copy(gu_hbm.at[0], gu, w_sem.at[1]),
        pltpu.make_async_copy(down_hbm.at[0], down, w_sem.at[2]),
    ]

    cache = [
        pltpu.make_async_copy(keys_hbm, keys_ref, w_sem.at[3]),
        pltpu.make_async_copy(values_hbm, values_ref, w_sem.at[4]),
    ]
    load_res = pltpu.make_async_copy(residual_hbm, r_all.at[par, half], w_sem.at[5])
    load_res.start()
    for load in cache:
        load.start()

    barrier = pltpu.get_barrier_semaphore()
    each(1, n, lambda k: pl.semaphore_signal(
        barrier, inc=1, device_id={"ctx": lax.rem(me + k, n)}, device_id_type=MESH))

    qf = q_ref[...].astype(F32)
    width = GROUPS * HD
    q_all[par, half] = jnp.concatenate(
        [qf[:, v * width:(v + 1) * width] for v in range(KVH)], axis=0).astype(BF16)

    counts = counts_ref[...].astype(F32)

    def slot_info(index, owner, place):
        lane = lax.broadcasted_iota(jnp.int32, (index, n), 1)
        start = jnp.sum(jnp.where(lane < owner, counts, 0.0), axis=1, keepdims=True)
        held = jnp.sum(jnp.where(lane == owner, counts, 0.0), axis=1, keepdims=True)
        return start, place.astype(F32) < held

    own_place = lax.broadcasted_iota(jnp.int32, (cap, 1), 0)
    _, own_valid = slot_info(cap, jnp.zeros((cap, 1), jnp.int32) + me, own_place)

    def upright(flat):
        return jnp.concatenate([flat, jnp.zeros((TOPK, LANES - cap), F32)], axis=1).T[:cap]

    ids = upright(ids_ref[...].astype(F32)).astype(jnp.int32)
    route = upright(route_ref[...])
    route = route / jnp.sum(route, axis=1, keepdims=True)
    expert_lane = lax.broadcasted_iota(jnp.int32, (cap, c_all.shape[-1]), 1)
    mixw = jnp.zeros((cap, c_all.shape[-1]), F32)
    for k in range(TOPK):
        mixw = mixw + jnp.where(expert_lane == ids[:, k:k + 1], route[:, k:k + 1], 0.0)
    c_all[par, half] = jnp.where(own_valid, mixw, 0.0)

    pl.semaphore_wait(barrier, n - 1)

    def z_peer(k):
        return lax.rem(z + k, nz) * ny + y

    def y_peer(k):
        return lax.rem(z + k, nz) * ny + (ny - 1 - y)

    def block_copy(buf, pa, h, sem, rs, dev):
        block = buf.at[pa, h]
        return remote(block, block, sem, rs.at[pa, h], dev)

    def gather_start(buf, sems):
        ss, ys, fs, rs = sems
        each(1, nz, lambda k: block_copy(
            buf, par, half, ss.at[k], rs, z_peer(k) * 2 + par).start())
        if ny > 1:
            block_copy(buf, par, half, ys.at[0], rs, y_peer(0) * 2 + par).start()
        block_copy(buf, par, half, ss.at[0], rs, sib).start()

    def pass_on(buf, sems, h):
        ss, ys, fs, rs = sems
        block_copy(buf, par, h, ss.at[0], rs, sib).wait_recv()
        block_copy(buf, par, h, fs.at[h], rs, sib).start()

    def gather_z(buf, sems):
        ss, ys, fs, rs = sems
        if ny > 1:
            pass_on(buf, sems, y_peer(0))

        def step(k):
            h = z_peer(nz - k)
            pass_on(buf, sems, h)
            if ny > 1:
                block_copy(buf, par, h, ys.at[k], rs, y_peer(0) * 2 + par).start()
        each(1, nz, step)

    def gather_y(buf, sems):
        if ny > 1:
            each(1, nz, lambda k: pass_on(buf, sems, y_peer(nz - k)))

    def gather_finish(buf, sems):
        ss, ys, fs, rs = sems
        each(0, half_n, lambda h: block_copy(
            buf, other, h, ss.at[0], rs, sib).wait_recv())

    def gather_drain(buf, sems):
        ss, ys, fs, rs = sems
        each(0, nz, lambda k: block_copy(buf, par, half, ss.at[k], rs, sib).wait_send())
        if ny > 1:
            each(0, nz, lambda k: block_copy(buf, par, half, ys.at[k], rs, sib).wait_send())
        each(1, half_n, lambda k: block_copy(
            buf, par, peer(k), fs.at[peer(k)], rs, sib).wait_send())

    q_g = (q_s, q_y, q_f, q_r)
    c_g = (c_s, c_y, c_f, c_r)
    r_g = (r_s, r_y, r_f, r_r)
    n_g = (n_s, n_y, n_f, n_r)
    gather_start(q_all, q_g)
    for load in loads:
        load.start()

    index = lax.broadcasted_iota(jnp.int32, (slots, 1), 0)
    block_of = index // cap
    owner = lax.rem(block_of, half_n) * 2 + block_of // half_n
    place = lax.rem(index, cap)
    start, filled = slot_info(slots, owner, place)
    at = start + place.astype(F32)
    row_lane = lax.broadcasted_iota(jnp.int32, (slots, rows), 1).astype(F32)
    order = order_ref[...].astype(F32)
    row_of = jnp.sum(jnp.where(row_lane == at, order, 0.0), axis=1, keepdims=True)
    row_of = jnp.where(filled, row_of, -1.0)
    pick = (row_lane == row_of).astype(BF16)
    lane = lax.broadcasted_iota(jnp.int32, (slots, rows), 1)
    block_lane = lane // home
    device_lane = lax.rem(block_lane, half_n) * 2 + block_lane // half_n
    row_lane = (device_lane * home + lax.rem(lane, home)).astype(F32)
    pick_par = (row_lane == row_of).astype(BF16)
    own_lane = me * home + lax.broadcasted_iota(jnp.int32, (slots, LANES), 1)
    pick_own = (own_lane.astype(F32) == row_of).astype(BF16)

    gather_z(q_all, q_g)
    gather_y(q_all, q_g)
    gather_finish(q_all, q_g)
    gather_start(c_all, c_g)
    load_res.wait()
    gather_start(r_all, r_g)
    for load in cache:
        load.wait()

    first_key = me * span
    per_head = HD // chunk
    pair = 2
    for request in range(requests):
        length = lengths[:, request:request + 1]
        blocks = STRETCH // home
        lo = request * blocks
        q_req = jnp.stack(
            [q_all[(lo + b) % 2, (lo + b) // 2]
             for b in range(blocks)], axis=0).astype(F32)
        q_req = q_req.reshape(blocks, KVH, home, width)
        key_pos = first_key + lax.broadcasted_iota(jnp.int32, (span, pair * STRETCH), 0)
        row_pos = length - STRETCH + lax.rem(
            lax.broadcasted_iota(jnp.int32, (span, pair * STRETCH), 1), STRETCH)
        allowed = key_pos <= row_pos
        for v in range(KVH):
            key_v = keys_ref[request, :, v * HD:(v + 1) * HD]
            val_v = values_ref[request, :, v * HD:(v + 1) * HD]
            val_t = val_v.astype(F32).T.astype(BF16)
            q_v = q_req[:, v].reshape(STRETCH, width)
            for g in range(0, GROUPS, pair):
                q_pair = jnp.concatenate(
                    [q_v[:, (g + i) * HD:(g + i + 1) * HD] for i in range(pair)],
                    axis=0).astype(BF16)
                scores = jnp.where(allowed, dot(key_v, q_pair, 1, 1), -1e30)
                top = jnp.max(scores, axis=0, keepdims=True)
                some = top > -1e29
                weights = jnp.exp2((scores - top) * (HD ** (-0.5) * LOG2E))
                total = jnp.where(some, jnp.sum(weights, axis=0, keepdims=True), 0.0)
                mixed = dot(val_t, weights.astype(BF16), 1, 0)
                mixed = jnp.where(some, mixed, 0.0).astype(BF16)
                top = jnp.where(some, top * HD ** (-0.5), -1e30)
                for i in range(pair):
                    head = v * GROUPS + g + i
                    cols = slice(request * STRETCH, (request + 1) * STRETCH)
                    take = slice(i * STRETCH, (i + 1) * STRETCH)
                    for c in range(per_head):
                        j = head * per_head + c
                        mix_snd[j % 2, j // 2, :, cols] = mixed[c * chunk:(c + 1) * chunk, take]
                        st_snd[j % 2, 0, j // 2:j // 2 + 1, cols] = top[:, take]
                        st_snd[j % 2, 1, j // 2:j // 2 + 1, cols] = total[:, take]

    x_mix = remote(mix_snd.at[other], mix_rcv, pair_s.at[0], pair_r.at[0], sib)
    x_st = remote(st_snd.at[other], st_rcv, pair_s.at[1], pair_r.at[1], sib)
    x_st.start()
    x_mix.start()
    gather_z(c_all, c_g)
    x_st.wait()
    x_mix.wait()
    top_a, top_b = st_snd[par, 0], st_rcv[0]
    best = jnp.maximum(top_a, top_b)
    fac_a, fac_b = jnp.exp(top_a - best), jnp.exp(top_b - best)
    total = st_snd[par, 1] * fac_a + st_rcv[1] * fac_b
    for q in range(half_n):
        s_snd[q, 0:1] = best[q:q + 1]
        s_snd[q, 1:2] = total[q:q + 1]
        m_snd[q] = (mix_snd[par, q].astype(F32) * fac_a[q:q + 1]
                    + mix_rcv[q].astype(F32) * fac_b[q:q + 1]).astype(BF16)

    def part_copies(k):
        p = peer(k)
        dev = p * 2 + par
        return (
            remote(s_snd.at[p], s_in.at[half], s_s.at[k], s_r.at[half], dev),
            remote(m_snd.at[p], m_in.at[half], m_s.at[k], m_r.at[half], dev),
        )

    def start_parts(k):
        for c in part_copies(k):
            c.start()

    each(1, half_n, start_parts)
    gather_y(c_all, c_g)
    gather_z(r_all, r_g)
    s_in[half, 0:2] = s_snd[half, 0:2]
    m_in[half] = m_snd[half]
    loads[0].wait()

    def wait_parts(k):
        p = peer(k)
        remote(s_snd.at[p], s_in.at[p], s_s.at[k], s_r.at[p], sib).wait_recv()
        remote(m_snd.at[p], m_in.at[p], m_s.at[k], m_r.at[p], sib).wait_recv()

    each(1, half_n, wait_parts)
    best = s_in[0, 0:1]
    for q in range(1, half_n):
        best = jnp.maximum(best, s_in[q, 0:1])
    denom = jnp.zeros_like(best)
    numer = jnp.zeros((chunk, rows), F32)
    for q in range(half_n):
        factor = jnp.exp(s_in[q, 0:1] - best)
        denom = denom + factor * s_in[q, 1:2]
        numer = numer + m_in[q].astype(F32) * factor
    attn = (numer / denom).astype(BF16)

    a_slots = dot(pick, attn, 1, 1).astype(BF16)
    a_snd[...] = a_slots.reshape(2, half_n, cap, chunk)

    def attn_copy(k):
        to = lax.rem(me + k, n)
        return remote(a_snd.at[lax.rem(to, 2), to // 2], a_in.at[me],
                      a_s.at[k], a_r.at[me], to)

    part = dot(attn, ow[...], 0, 0)
    wide = D // 2
    for d in range(n):
        own = part[d * home:(d + 1) * home]
        p_snd[d % 2, d // 2] = jnp.concatenate(
            [own[:, :wide], own[:, wide:]], axis=0).astype(BF16)
    x_p = remote(p_snd.at[other], p_rcv, pair_s.at[2], pair_r.at[2], sib)
    x_p.start()
    gather_y(r_all, r_g)
    x_p.wait()

    def spread_y(mine, got, mid, into, yin, ss, ys, rs, yr):
        if ny > 1:
            def step_y(k):
                h = y_peer(k)
                to = h // ny
                mid[h] = (mine[par, h].astype(F32) + got[h].astype(F32)).astype(BF16)
                remote(mid.at[h], yin.at[to], ys.at[k - 1], yr.at[to],
                       y_peer(0) * 2 + par).start()
            each(1, nz + 1, step_y)

    def spread_z(mine, got, mid, into, yin, ss, ys, rs, yr):
        def step(k):
            h = z_peer(k)
            total = mine[par, h].astype(F32) + got[h].astype(F32)
            if ny > 1:
                to = h // ny
                remote(mid.at[h], yin.at[to], ss.at[k], yr.at[to], sib).wait_recv()
                total = total + yin[to].astype(F32)
            mid[h] = total.astype(BF16)
            remote(mid.at[h], into.at[z], ss.at[k], rs.at[z], h * 2 + par).start()
        each(1, nz, step)

    def collect(mine, got, mid, into, yin, ss, ys, rs, yr):
        total = mine[par, half].astype(F32) + got[half].astype(F32)
        if ny > 1:
            remote(mid.at[0], yin.at[z], ss.at[0], yr.at[z], sib).wait_recv()
            total = total + yin[z].astype(F32)

        def step(k, total):
            at_z = lax.rem(z - k + nz, nz)
            remote(mid.at[0], into.at[at_z], ss.at[k], rs.at[at_z], sib).wait_recv()
            return total + into[at_z].astype(F32)
        return lax.fori_loop(1, nz, step, total)

    def drain_spread(mid, into, yin, ss, ys, rs, yr):
        each(1, nz, lambda k: remote(
            mid.at[0], into.at[0], ss.at[k], rs.at[0], sib).wait_send())
        if ny > 1:
            each(0, nz, lambda k: remote(
                mid.at[0], yin.at[0], ys.at[k], yr.at[0], sib).wait_send())

    p_x = (p_mid, p_in, p_yin, p_s, p_y, p_r, p_yr)
    e_x = [[ref.at[i] for ref in (
        e_snd, e_rcv, e_mid, e_in, e_yin, e_s, e_y, e_r, e_yr)] for i in range(2)]
    spread_y(p_snd, p_rcv, *p_x)
    spread_z(p_snd, p_rcv, *p_x)

    gather_finish(r_all, r_g)
    held = dot(pick_own, r_all[...].reshape(slots, D), 0, 0)[:home]
    held = jnp.concatenate([held[:, :wide], held[:, wide:]], axis=0)
    projected = collect(p_snd, p_rcv, *p_x)
    stream = (held + projected).astype(BF16).astype(F32)
    square = jnp.sum(stream * stream, axis=1, keepdims=True)
    scale = lax.rsqrt((square[:home] + square[home:]) / D + 1e-06)
    gain = gain_ref[...]
    gain = jnp.concatenate(
        [jnp.broadcast_to(gain[:, :wide], (home, wide)),
         jnp.broadcast_to(gain[:, wide:], (home, wide))], axis=0)
    normed = stream * jnp.concatenate([scale, scale], axis=0) * gain
    n_all[par, half] = normed.astype(BF16)
    gather_start(n_all, n_g)
    blank = jnp.zeros((LANES - home, D), F32)
    str_buf[...] = jnp.concatenate(
        [jnp.concatenate([stream[:home], stream[home:]], axis=1), blank], axis=0).astype(BF16)
    gather_finish(c_all, c_g)
    loads[1].wait()
    loads[2].wait()
    gather_z(n_all, n_g)
    gather_y(n_all, n_g)

    def repack(parity):
        halves = n_all[parity].astype(F32).reshape(half_n, 2, home, wide)
        x_buf[parity, :, :wide] = halves[:, 0].reshape(rows // 2, wide).astype(BF16)
        x_buf[parity, :, wide:] = halves[:, 1].reshape(rows // 2, wide).astype(BF16)

    repack(par)
    gather_finish(n_all, n_g)
    repack(other)

    lane = lax.broadcasted_iota(jnp.int32, (slots, c_all.shape[-1]), 1)
    tile = 256
    each(1, n, lambda k: attn_copy(k).start())

    x = x_buf.reshape(rows, D)

    def up(t, c):
        lo = pl.multiple_of(t * tile, tile)
        gate = dot(x[...], gu[:, pl.ds(lo, tile)], 1, 0)
        lift = dot(x[...], gu[:, pl.ds(EFF + lo, tile)], 1, 0)
        hid[:, pl.ds(lo, tile)] = (gate / (1.0 + jnp.exp(-gate)) * lift).astype(BF16)
        return c
    lax.fori_loop(0, EFF // tile, up, 0)
    routes = c_all[...].reshape(slots, c_all.shape[-1])
    weight = jnp.sum(jnp.where(lane == me, routes, 0.0), axis=1, keepdims=True)

    side = D // 2

    def lower(i, first, last):
        def step(t, c):
            lo = pl.multiple_of(t * tile, tile)
            cols = pl.ds(pl.multiple_of(i * side + lo, tile), tile)
            result = dot(hid[...], down[:, cols], 1, 0).astype(BF16)
            part = dot(pick_par, result, 1, 0) * weight
            part = part + dot(pick_own, str_buf[:, cols], 1, 0)
            e_snd[i, :, :, :, pl.ds(lo, tile)] = part.astype(BF16).reshape(
                2, half_n, cap, tile)
            return c
        lax.fori_loop(first, last, step, 0)

    x_e = [remote(e_snd.at[i, other], e_rcv.at[i], pair_s.at[3 + i], pair_r.at[3 + i], sib)
           for i in range(2)]
    tiles = side // tile
    lower(0, 0, tiles)
    x_e[0].start()
    lower(1, 0, tiles // 2)
    x_e[0].wait()
    spread_y(*e_x[0])
    lower(1, tiles // 2, tiles)
    x_e[1].start()
    spread_z(*e_x[0])
    x_e[1].wait()
    spread_y(*e_x[1])
    spread_z(*e_x[1])

    a_in[me] = a_snd[par, half]

    def wait_attn(k):
        at_k = lax.rem(me + k, n)
        remote(a_snd.at[0, 0], a_in.at[at_k], a_s.at[k], a_r.at[at_k], sib).wait_recv()

    each(1, n, wait_attn)
    out[0] = jnp.concatenate([a_in[j] for j in range(n)], axis=1)

    moe = jnp.concatenate([collect(*e_x[i]) for i in range(2)], axis=1)
    out[1] = jnp.where(own_valid, moe, 0.0).astype(BF16)

    def drain(k):
        for c in part_copies(k):
            c.wait_send()

    each(1, half_n, drain)
    drain_spread(*p_x)
    drain_spread(*e_x[0][2:])
    drain_spread(*e_x[1][2:])
    gather_drain(q_all, q_g)
    gather_drain(c_all, c_g)
    gather_drain(r_all, r_g)
    gather_drain(n_all, n_g)
    each(1, n, lambda k: attn_copy(k).wait_send())


def body(
    queries,
    keys,
    values,
    lengths,
    owner_counts,
    row_order,
    residual,
    out_weight,
    norm_gain,
    expert_ids,
    route_weights,
    gate_up,
    expert_down,
):
    n = lax.axis_size("ctx")
    half_n = n // 2
    home = queries.shape[0]
    rows = n * home
    cap = residual.shape[0]
    chunk = out_weight.shape[0]
    lanes = -(-n // LANES) * LANES
    vmem = pl.BlockSpec(memory_space=pltpu.VMEM)
    anywhere = pl.BlockSpec(memory_space=pl.ANY)
    dma = pltpu.SemaphoreType.DMA
    slot_block = (half_n, cap, D)
    ny = 2 if half_n % 2 == 0 else 1
    nz = half_n // ny
    side_block = (half_n, cap, D // 2)
    row_block = (half_n, 2 * home, D // 2)
    scratch = [
        pltpu.VMEM(keys.shape, BF16),
        pltpu.VMEM(values.shape, BF16),
        pltpu.VMEM(out_weight.shape, BF16),
        pltpu.VMEM(gate_up.shape[1:], BF16),
        pltpu.VMEM(expert_down.shape[1:], BF16),
        pltpu.VMEM((2, half_n, KVH * home, GROUPS * HD), BF16),
        pltpu.VMEM((2, half_n, cap, lanes), F32),
        pltpu.VMEM((2, half_n, chunk, rows), BF16),
        pltpu.VMEM((2, 2, half_n, rows), F32),
        pltpu.VMEM((half_n, chunk, rows), BF16),
        pltpu.VMEM((2, half_n, rows), F32),
        pltpu.VMEM((half_n, chunk, rows), BF16),
        pltpu.VMEM((half_n, 8, rows), F32),
        pltpu.VMEM((half_n, chunk, rows), BF16),
        pltpu.VMEM((half_n, 8, rows), F32),
        pltpu.VMEM((2, half_n, cap, chunk), BF16),
        pltpu.VMEM((n, cap, chunk), BF16),
        pltpu.VMEM((2,) + row_block, BF16),
        pltpu.VMEM(row_block, BF16),
        pltpu.VMEM(row_block, BF16),
        pltpu.VMEM((nz,) + row_block[1:], BF16),
        pltpu.VMEM((nz,) + row_block[1:], BF16),
        pltpu.VMEM((2,) + slot_block, BF16),
        pltpu.VMEM((2,) + row_block, BF16),
        pltpu.VMEM((2, rows // 2, D), BF16),
        pltpu.VMEM((LANES, D), BF16),
        pltpu.VMEM((rows, EFF), BF16),
        pltpu.VMEM((2, 2) + side_block, BF16),
        pltpu.VMEM((2,) + side_block, BF16),
        pltpu.VMEM((2,) + side_block, BF16),
        pltpu.VMEM((2, nz) + side_block[1:], BF16),
        pltpu.VMEM((2, nz) + side_block[1:], BF16),
        dma((6,)),
    ]
    gather = [dma((nz,)), dma((nz,)), dma((half_n,)), dma((2, half_n))]
    exchange = [dma((half_n,)), dma((half_n,))]
    staged = [dma((nz,)), dma((nz,)), dma((nz,)), dma((nz,))]
    scratch += gather + gather
    scratch += [dma((5,)), dma((5,))]
    scratch += exchange + exchange
    scratch += [dma((n,)), dma((n,))]
    scratch += staged + gather + gather + [dma((2, nz))] * 4
    out = pl.pallas_call(
        functools.partial(kernel, n),
        out_shape=jax.ShapeDtypeStruct((2, cap, D), BF16),
        in_specs=[vmem] * 4 + [anywhere] * 3 + [vmem] * 3 + [anywhere] * 3,
        out_specs=vmem,
        scratch_shapes=scratch,
        compiler_params=pltpu.CompilerParams(
            collective_id=0, has_side_effects=True, vmem_limit_bytes=60 * 2**20
        ),
    )(
        lengths.reshape(1, keys.shape[0]),
        owner_counts.reshape(1, n),
        row_order.reshape(1, rows),
        queries,
        keys,
        values,
        residual,
        expert_ids.T,
        route_weights.T,
        norm_gain.reshape(1, D),
        out_weight,
        gate_up,
        expert_down,
    )
    return out[0], out[1]


def solution(mesh):
    placed = (
        P(("groups", "ctx"), None),
        P("groups", "ctx", None),
        P("groups", "ctx", None),
        P("groups"),
        P("groups"),
        P("groups"),
        P(("groups", "ctx"), None),
        P("ctx", None),
        P(),
        P(("groups", "ctx"), None),
        P(("groups", "ctx"), None),
        P("ctx", None, None),
        P("ctx", None, None),
    )
    return jax.shard_map(
        body,
        mesh=mesh,
        in_specs=placed,
        out_specs=(P(("groups", "ctx"), None), P(("groups", "ctx"), None)),
        check_vma=False,
    )
```

```python
import functools

import jax
import jax.numpy as jnp
from jax import lax
from jax.experimental import pallas as pl
from jax.experimental.pallas import tpu as pltpu
from jax.sharding import PartitionSpec as P

D = 2048
HQ = 16
KVH = 2
HD = 128
EFF = 768
TOPK = 8
STRETCH = 128
GROUPS = HQ // KVH
LANES = 128
LOG2E = 1.4426950408889634
F32 = jnp.float32
BF16 = jnp.bfloat16
MESH = pl.DeviceIdType.MESH


def dot(a, b, ca, cb):
    return lax.dot_general(a, b, (((ca,), (cb,)), ((), ())), preferred_element_type=F32)


def kernel(
    n,
    lengths,
    counts_ref,
    order_ref,
    q_ref,
    keys_hbm,
    values_hbm,
    residual_hbm,
    ids_ref,
    route_ref,
    gain_ref,
    ow_hbm,
    gu_hbm,
    down_hbm,
    out,
    keys_ref,
    values_ref,
    ow,
    gu,
    down,
    q_all,
    c_all,
    mix_snd,
    st_snd,
    mix_rcv,
    st_rcv,
    m_snd,
    s_snd,
    m_in,
    s_in,
    a_snd,
    a_in,
    p_snd,
    p_rcv,
    p_mid,
    p_in,
    p_yin,
    r_all,
    n_all,
    x_buf,
    str_buf,
    hid,
    e_snd,
    e_rcv,
    e_mid,
    e_in,
    e_yin,
    w_sem,
    q_s,
    q_y,
    q_f,
    q_r,
    c_s,
    c_y,
    c_f,
    c_r,
    pair_s,
    pair_r,
    m_s,
    m_r,
    s_s,
    s_r,
    a_s,
    a_r,
    p_s,
    p_y,
    p_r,
    p_yr,
    r_s,
    r_y,
    r_f,
    r_r,
    n_s,
    n_y,
    n_f,
    n_r,
    e_s,
    e_y,
    e_r,
    e_yr,
):
    half_n = n // 2
    home = q_ref.shape[0]
    rows = n * home
    cap = residual_hbm.shape[0]
    slots = n * cap
    chunk = ow.shape[0]
    span = keys_ref.shape[1]
    requests = keys_ref.shape[0]
    me = lax.axis_index("ctx")
    par = lax.rem(me, 2)
    half = me // 2
    other = 1 - par
    sib = half * 2 + other

    ny = 2 if half_n % 2 == 0 else 1
    nz = half_n // ny
    z, y = half // ny, lax.rem(half, ny)

    def peer(k):
        return lax.rem(half + k, half_n)

    def remote(src, dst, ss, rs, dev):
        return pltpu.make_async_remote_copy(
            src_ref=src, dst_ref=dst, send_sem=ss, recv_sem=rs,
            device_id={"ctx": dev}, device_id_type=MESH,
        )

    def each(lo, hi, f):
        def step(k, c):
            f(k)
            return c
        lax.fori_loop(lo, hi, step, 0)

    loads = [
        pltpu.make_async_copy(ow_hbm, ow, w_sem.at[0]),
        pltpu.make_async_copy(gu_hbm.at[0], gu, w_sem.at[1]),
        pltpu.make_async_copy(down_hbm.at[0], down, w_sem.at[2]),
    ]

    cache = [
        pltpu.make_async_copy(keys_hbm, keys_ref, w_sem.at[3]),
        pltpu.make_async_copy(values_hbm, values_ref, w_sem.at[4]),
    ]
    load_res = pltpu.make_async_copy(residual_hbm, r_all.at[par, half], w_sem.at[5])
    load_res.start()
    for load in cache:
        load.start()

    barrier = pltpu.get_barrier_semaphore()
    each(1, n, lambda k: pl.semaphore_signal(
        barrier, inc=1, device_id={"ctx": lax.rem(me + k, n)}, device_id_type=MESH))

    qf = q_ref[...].astype(F32)
    width = GROUPS * HD
    q_all[par, half] = jnp.concatenate(
        [qf[:, v * width:(v + 1) * width] for v in range(KVH)], axis=0).astype(BF16)

    counts = counts_ref[...].astype(F32)

    def slot_info(index, owner, place):
        lane = lax.broadcasted_iota(jnp.int32, (index, n), 1)
        start = jnp.sum(jnp.where(lane < owner, counts, 0.0), axis=1, keepdims=True)
        held = jnp.sum(jnp.where(lane == owner, counts, 0.0), axis=1, keepdims=True)
        return start, place.astype(F32) < held

    own_place = lax.broadcasted_iota(jnp.int32, (cap, 1), 0)
    _, own_valid = slot_info(cap, jnp.zeros((cap, 1), jnp.int32) + me, own_place)

    def upright(flat):
        return jnp.concatenate([flat, jnp.zeros((TOPK, LANES - cap), F32)], axis=1).T[:cap]

    ids = upright(ids_ref[...].astype(F32)).astype(jnp.int32)
    route = upright(route_ref[...])
    route = route / jnp.sum(route, axis=1, keepdims=True)
    expert_lane = lax.broadcasted_iota(jnp.int32, (cap, c_all.shape[-1]), 1)
    mixw = jnp.zeros((cap, c_all.shape[-1]), F32)
    for k in range(TOPK):
        mixw = mixw + jnp.where(expert_lane == ids[:, k:k + 1], route[:, k:k + 1], 0.0)
    c_all[par, half] = jnp.where(own_valid, mixw, 0.0)

    pl.semaphore_wait(barrier, n - 1)

    def z_to(k):
        k = lax.rem(k, nz)
        if nz & (nz - 1):
            return lax.rem(z + k, nz)
        to, bit = 0, 1
        while bit < nz:
            to = to + lax.rem(z // bit + k // bit, 2) * bit
            bit = bit * 2
        return to

    def z_peer(k):
        return z_to(k) * ny + y

    def y_peer(k):
        return z_to(k) * ny + (ny - 1 - y)

    z_own_y = z * ny + (ny - 1 - y)

    def block_copy(buf, pa, h, sem, rs, dev):
        block = buf.at[pa, h]
        return remote(block, block, sem, rs.at[pa, h], dev)

    def gather_start(buf, sems):
        ss, ys, fs, rs = sems
        each(1, nz, lambda k: block_copy(
            buf, par, half, ss.at[k], rs, z_peer(k) * 2 + par).start())
        if ny > 1:
            block_copy(buf, par, half, ys.at[0], rs, z_own_y * 2 + par).start()
        block_copy(buf, par, half, ss.at[0], rs, sib).start()

    def pass_on(buf, sems, h):
        ss, ys, fs, rs = sems
        block_copy(buf, par, h, ss.at[0], rs, sib).wait_recv()
        block_copy(buf, par, h, fs.at[h], rs, sib).start()

    def gather_z(buf, sems):
        ss, ys, fs, rs = sems
        if ny > 1:
            pass_on(buf, sems, z_own_y)

        def step(k):
            h = z_peer(k)
            pass_on(buf, sems, h)
            if ny > 1:
                block_copy(buf, par, h, ys.at[k], rs, z_own_y * 2 + par).start()
        each(1, nz, step)

    def gather_y(buf, sems):
        if ny > 1:
            each(1, nz, lambda k: pass_on(buf, sems, y_peer(k)))

    def gather_finish(buf, sems):
        ss, ys, fs, rs = sems
        each(0, half_n, lambda h: block_copy(
            buf, other, h, ss.at[0], rs, sib).wait_recv())

    def gather_drain(buf, sems):
        ss, ys, fs, rs = sems
        each(0, nz, lambda k: block_copy(buf, par, half, ss.at[k], rs, sib).wait_send())
        if ny > 1:
            each(0, nz, lambda k: block_copy(buf, par, half, ys.at[k], rs, sib).wait_send())
        each(1, half_n, lambda k: block_copy(
            buf, par, peer(k), fs.at[peer(k)], rs, sib).wait_send())

    q_g = (q_s, q_y, q_f, q_r)
    c_g = (c_s, c_y, c_f, c_r)
    r_g = (r_s, r_y, r_f, r_r)
    n_g = (n_s, n_y, n_f, n_r)
    gather_start(q_all, q_g)
    for load in loads:
        load.start()

    index = lax.broadcasted_iota(jnp.int32, (slots, 1), 0)
    block_of = index // cap
    owner = lax.rem(block_of, half_n) * 2 + block_of // half_n
    place = lax.rem(index, cap)
    start, filled = slot_info(slots, owner, place)
    at = start + place.astype(F32)
    row_lane = lax.broadcasted_iota(jnp.int32, (slots, rows), 1).astype(F32)
    order = order_ref[...].astype(F32)
    row_of = jnp.sum(jnp.where(row_lane == at, order, 0.0), axis=1, keepdims=True)
    row_of = jnp.where(filled, row_of, -1.0)
    pick = (row_lane == row_of).astype(BF16)
    lane = lax.broadcasted_iota(jnp.int32, (slots, rows), 1)
    block_lane = lane // home
    device_lane = lax.rem(block_lane, half_n) * 2 + block_lane // half_n
    row_lane = (device_lane * home + lax.rem(lane, home)).astype(F32)
    pick_par = (row_lane == row_of).astype(BF16)
    own_lane = me * home + lax.broadcasted_iota(jnp.int32, (slots, LANES), 1)
    pick_own = (own_lane.astype(F32) == row_of).astype(BF16)

    gather_z(q_all, q_g)
    gather_y(q_all, q_g)
    gather_finish(q_all, q_g)
    gather_start(c_all, c_g)
    load_res.wait()
    gather_start(r_all, r_g)
    for load in cache:
        load.wait()

    first_key = me * span
    per_head = HD // chunk
    pair = 2
    for request in range(requests):
        length = lengths[:, request:request + 1]
        blocks = STRETCH // home
        lo = request * blocks
        q_req = jnp.stack(
            [q_all[(lo + b) % 2, (lo + b) // 2]
             for b in range(blocks)], axis=0).astype(F32)
        q_req = q_req.reshape(blocks, KVH, home, width)
        key_pos = first_key + lax.broadcasted_iota(jnp.int32, (span, pair * STRETCH), 0)
        row_pos = length - STRETCH + lax.rem(
            lax.broadcasted_iota(jnp.int32, (span, pair * STRETCH), 1), STRETCH)
        allowed = key_pos <= row_pos
        for v in range(KVH):
            key_v = keys_ref[request, :, v * HD:(v + 1) * HD]
            val_v = values_ref[request, :, v * HD:(v + 1) * HD]
            val_t = val_v.astype(F32).T.astype(BF16)
            q_v = q_req[:, v].reshape(STRETCH, width)
            for g in range(0, GROUPS, pair):
                q_pair = jnp.concatenate(
                    [q_v[:, (g + i) * HD:(g + i + 1) * HD] for i in range(pair)],
                    axis=0).astype(BF16)
                scores = jnp.where(allowed, dot(key_v, q_pair, 1, 1), -1e30)
                top = jnp.max(scores, axis=0, keepdims=True)
                some = top > -1e29
                weights = jnp.exp2((scores - top) * (HD ** (-0.5) * LOG2E))
                total = jnp.where(some, jnp.sum(weights, axis=0, keepdims=True), 0.0)
                mixed = dot(val_t, weights.astype(BF16), 1, 0)
                mixed = jnp.where(some, mixed, 0.0).astype(BF16)
                top = jnp.where(some, top * HD ** (-0.5), -1e30)
                for i in range(pair):
                    head = v * GROUPS + g + i
                    cols = slice(request * STRETCH, (request + 1) * STRETCH)
                    take = slice(i * STRETCH, (i + 1) * STRETCH)
                    for c in range(per_head):
                        j = head * per_head + c
                        mix_snd[j % 2, j // 2, :, cols] = mixed[c * chunk:(c + 1) * chunk, take]
                        st_snd[j % 2, 0, j // 2:j // 2 + 1, cols] = top[:, take]
                        st_snd[j % 2, 1, j // 2:j // 2 + 1, cols] = total[:, take]

    x_mix = remote(mix_snd.at[other], mix_rcv, pair_s.at[0], pair_r.at[0], sib)
    x_st = remote(st_snd.at[other], st_rcv, pair_s.at[1], pair_r.at[1], sib)
    x_st.start()
    x_mix.start()
    gather_z(c_all, c_g)
    x_st.wait()
    x_mix.wait()
    top_a, top_b = st_snd[par, 0], st_rcv[0]
    best = jnp.maximum(top_a, top_b)
    fac_a, fac_b = jnp.exp(top_a - best), jnp.exp(top_b - best)
    total = st_snd[par, 1] * fac_a + st_rcv[1] * fac_b
    for q in range(half_n):
        s_snd[q, 0:1] = best[q:q + 1]
        s_snd[q, 1:2] = total[q:q + 1]
        m_snd[q] = (mix_snd[par, q].astype(F32) * fac_a[q:q + 1]
                    + mix_rcv[q].astype(F32) * fac_b[q:q + 1]).astype(BF16)

    def part_copies(k):
        p = peer(k)
        dev = p * 2 + par
        return (
            remote(s_snd.at[p], s_in.at[half], s_s.at[k], s_r.at[half], dev),
            remote(m_snd.at[p], m_in.at[half], m_s.at[k], m_r.at[half], dev),
        )

    def start_parts(k):
        for c in part_copies(k):
            c.start()

    each(1, half_n, start_parts)
    gather_y(c_all, c_g)
    gather_z(r_all, r_g)
    s_in[half, 0:2] = s_snd[half, 0:2]
    m_in[half] = m_snd[half]
    loads[0].wait()

    def wait_parts(k):
        p = peer(k)
        remote(s_snd.at[p], s_in.at[p], s_s.at[k], s_r.at[p], sib).wait_recv()
        remote(m_snd.at[p], m_in.at[p], m_s.at[k], m_r.at[p], sib).wait_recv()

    each(1, half_n, wait_parts)
    best = s_in[0, 0:1]
    for q in range(1, half_n):
        best = jnp.maximum(best, s_in[q, 0:1])
    denom = jnp.zeros_like(best)
    numer = jnp.zeros((chunk, rows), F32)
    for q in range(half_n):
        factor = jnp.exp(s_in[q, 0:1] - best)
        denom = denom + factor * s_in[q, 1:2]
        numer = numer + m_in[q].astype(F32) * factor
    attn = (numer / denom).astype(BF16)

    a_slots = dot(pick, attn, 1, 1).astype(BF16)
    a_snd[...] = a_slots.reshape(2, half_n, cap, chunk)

    def attn_copy(k):
        to = lax.rem(me + k, n)
        return remote(a_snd.at[lax.rem(to, 2), to // 2], a_in.at[me],
                      a_s.at[k], a_r.at[me], to)

    part = dot(attn, ow[...], 0, 0)
    wide = D // 2
    for d in range(n):
        own = part[d * home:(d + 1) * home]
        p_snd[d % 2, d // 2] = jnp.concatenate(
            [own[:, :wide], own[:, wide:]], axis=0).astype(BF16)
    x_p = remote(p_snd.at[other], p_rcv, pair_s.at[2], pair_r.at[2], sib)
    x_p.start()
    gather_y(r_all, r_g)
    x_p.wait()

    def spread_y(mine, got, mid, into, yin, ss, ys, rs, yr):
        if ny > 1:
            def step_y(k):
                h = y_peer(nz - k)
                to = h // ny
                mid[h] = (mine[par, h].astype(F32) + got[h].astype(F32)).astype(BF16)
                remote(mid.at[h], yin.at[to], ys.at[k - 1], yr.at[to],
                       z_own_y * 2 + par).start()
            each(1, nz + 1, step_y)

    def spread_z(mine, got, mid, into, yin, ss, ys, rs, yr):
        def step(k):
            h = z_peer(nz - k)
            total = mine[par, h].astype(F32) + got[h].astype(F32)
            if ny > 1:
                to = h // ny
                remote(mid.at[h], yin.at[to], ss.at[k], yr.at[to], sib).wait_recv()
                total = total + yin[to].astype(F32)
            mid[h] = total.astype(BF16)
            remote(mid.at[h], into.at[z], ss.at[k], rs.at[z], h * 2 + par).start()
        each(1, nz, step)

    def collect(mine, got, mid, into, yin, ss, ys, rs, yr):
        total = mine[par, half].astype(F32) + got[half].astype(F32)
        if ny > 1:
            remote(mid.at[0], yin.at[z], ss.at[0], yr.at[z], sib).wait_recv()
            total = total + yin[z].astype(F32)

        def step(k, total):
            at_z = lax.rem(z - k + nz, nz)
            remote(mid.at[0], into.at[at_z], ss.at[k], rs.at[at_z], sib).wait_recv()
            return total + into[at_z].astype(F32)
        return lax.fori_loop(1, nz, step, total)

    def drain_spread(mid, into, yin, ss, ys, rs, yr):
        each(1, nz, lambda k: remote(
            mid.at[0], into.at[0], ss.at[k], rs.at[0], sib).wait_send())
        if ny > 1:
            each(0, nz, lambda k: remote(
                mid.at[0], yin.at[0], ys.at[k], yr.at[0], sib).wait_send())

    p_x = (p_mid, p_in, p_yin, p_s, p_y, p_r, p_yr)
    e_x = [[ref.at[i] for ref in (
        e_snd, e_rcv, e_mid, e_in, e_yin, e_s, e_y, e_r, e_yr)] for i in range(2)]
    spread_y(p_snd, p_rcv, *p_x)
    spread_z(p_snd, p_rcv, *p_x)

    gather_finish(r_all, r_g)
    held = dot(pick_own, r_all[...].reshape(slots, D), 0, 0)[:home]
    held = jnp.concatenate([held[:, :wide], held[:, wide:]], axis=0)
    projected = collect(p_snd, p_rcv, *p_x)
    stream = (held + projected).astype(BF16).astype(F32)
    square = jnp.sum(stream * stream, axis=1, keepdims=True)
    scale = lax.rsqrt((square[:home] + square[home:]) / D + 1e-06)
    gain = gain_ref[...]
    gain = jnp.concatenate(
        [jnp.broadcast_to(gain[:, :wide], (home, wide)),
         jnp.broadcast_to(gain[:, wide:], (home, wide))], axis=0)
    normed = stream * jnp.concatenate([scale, scale], axis=0) * gain
    n_all[par, half] = normed.astype(BF16)
    gather_start(n_all, n_g)
    blank = jnp.zeros((LANES - home, D), F32)
    str_buf[...] = jnp.concatenate(
        [jnp.concatenate([stream[:home], stream[home:]], axis=1), blank], axis=0).astype(BF16)
    gather_finish(c_all, c_g)
    loads[1].wait()
    loads[2].wait()
    gather_z(n_all, n_g)
    gather_y(n_all, n_g)

    def repack(parity):
        halves = n_all[parity].astype(F32).reshape(half_n, 2, home, wide)
        x_buf[parity, :, :wide] = halves[:, 0].reshape(rows // 2, wide).astype(BF16)
        x_buf[parity, :, wide:] = halves[:, 1].reshape(rows // 2, wide).astype(BF16)

    repack(par)
    gather_finish(n_all, n_g)
    repack(other)

    lane = lax.broadcasted_iota(jnp.int32, (slots, c_all.shape[-1]), 1)
    tile = 256
    each(1, n, lambda k: attn_copy(k).start())

    x = x_buf.reshape(rows, D)

    def up(t, c):
        lo = pl.multiple_of(t * tile, tile)
        gate = dot(x[...], gu[:, pl.ds(lo, tile)], 1, 0)
        lift = dot(x[...], gu[:, pl.ds(EFF + lo, tile)], 1, 0)
        hid[:, pl.ds(lo, tile)] = (gate / (1.0 + jnp.exp(-gate)) * lift).astype(BF16)
        return c
    lax.fori_loop(0, EFF // tile, up, 0)
    routes = c_all[...].reshape(slots, c_all.shape[-1])
    weight = jnp.sum(jnp.where(lane == me, routes, 0.0), axis=1, keepdims=True)

    side = D // 2

    def lower(i, first, last):
        def step(t, c):
            lo = pl.multiple_of(t * tile, tile)
            cols = pl.ds(pl.multiple_of(i * side + lo, tile), tile)
            result = dot(hid[...], down[:, cols], 1, 0).astype(BF16)
            part = dot(pick_par, result, 1, 0) * weight
            part = part + dot(pick_own, str_buf[:, cols], 1, 0)
            e_snd[i, :, :, :, pl.ds(lo, tile)] = part.astype(BF16).reshape(
                2, half_n, cap, tile)
            return c
        lax.fori_loop(first, last, step, 0)

    x_e = [remote(e_snd.at[i, other], e_rcv.at[i], pair_s.at[3 + i], pair_r.at[3 + i], sib)
           for i in range(2)]
    tiles = side // tile
    lower(0, 0, tiles)
    x_e[0].start()
    lower(1, 0, tiles // 2)
    x_e[0].wait()
    spread_y(*e_x[0])
    lower(1, tiles // 2, tiles)
    x_e[1].start()
    x_e[1].wait()
    spread_y(*e_x[1])
    spread_z(*e_x[0])
    spread_z(*e_x[1])

    a_in[me] = a_snd[par, half]

    def wait_attn(k):
        at_k = lax.rem(me + k, n)
        remote(a_snd.at[0, 0], a_in.at[at_k], a_s.at[k], a_r.at[at_k], sib).wait_recv()

    each(1, n, wait_attn)
    out[0] = jnp.concatenate([a_in[j] for j in range(n)], axis=1)

    moe = jnp.concatenate([collect(*e_x[i]) for i in range(2)], axis=1)
    out[1] = jnp.where(own_valid, moe, 0.0).astype(BF16)

    def drain(k):
        for c in part_copies(k):
            c.wait_send()

    each(1, half_n, drain)
    drain_spread(*p_x)
    drain_spread(*e_x[0][2:])
    drain_spread(*e_x[1][2:])
    gather_drain(q_all, q_g)
    gather_drain(c_all, c_g)
    gather_drain(r_all, r_g)
    gather_drain(n_all, n_g)
    each(1, n, lambda k: attn_copy(k).wait_send())


def body(
    queries,
    keys,
    values,
    lengths,
    owner_counts,
    row_order,
    residual,
    out_weight,
    norm_gain,
    expert_ids,
    route_weights,
    gate_up,
    expert_down,
):
    n = lax.axis_size("ctx")
    half_n = n // 2
    home = queries.shape[0]
    rows = n * home
    cap = residual.shape[0]
    chunk = out_weight.shape[0]
    lanes = -(-n // LANES) * LANES
    vmem = pl.BlockSpec(memory_space=pltpu.VMEM)
    anywhere = pl.BlockSpec(memory_space=pl.ANY)
    dma = pltpu.SemaphoreType.DMA
    slot_block = (half_n, cap, D)
    ny = 2 if half_n % 2 == 0 else 1
    nz = half_n // ny
    side_block = (half_n, cap, D // 2)
    row_block = (half_n, 2 * home, D // 2)
    scratch = [
        pltpu.VMEM(keys.shape, BF16),
        pltpu.VMEM(values.shape, BF16),
        pltpu.VMEM(out_weight.shape, BF16),
        pltpu.VMEM(gate_up.shape[1:], BF16),
        pltpu.VMEM(expert_down.shape[1:], BF16),
        pltpu.VMEM((2, half_n, KVH * home, GROUPS * HD), BF16),
        pltpu.VMEM((2, half_n, cap, lanes), F32),
        pltpu.VMEM((2, half_n, chunk, rows), BF16),
        pltpu.VMEM((2, 2, half_n, rows), F32),
        pltpu.VMEM((half_n, chunk, rows), BF16),
        pltpu.VMEM((2, half_n, rows), F32),
        pltpu.VMEM((half_n, chunk, rows), BF16),
        pltpu.VMEM((half_n, 8, rows), F32),
        pltpu.VMEM((half_n, chunk, rows), BF16),
        pltpu.VMEM((half_n, 8, rows), F32),
        pltpu.VMEM((2, half_n, cap, chunk), BF16),
        pltpu.VMEM((n, cap, chunk), BF16),
        pltpu.VMEM((2,) + row_block, BF16),
        pltpu.VMEM(row_block, BF16),
        pltpu.VMEM(row_block, BF16),
        pltpu.VMEM((nz,) + row_block[1:], BF16),
        pltpu.VMEM((nz,) + row_block[1:], BF16),
        pltpu.VMEM((2,) + slot_block, BF16),
        pltpu.VMEM((2,) + row_block, BF16),
        pltpu.VMEM((2, rows // 2, D), BF16),
        pltpu.VMEM((LANES, D), BF16),
        pltpu.VMEM((rows, EFF), BF16),
        pltpu.VMEM((2, 2) + side_block, BF16),
        pltpu.VMEM((2,) + side_block, BF16),
        pltpu.VMEM((2,) + side_block, BF16),
        pltpu.VMEM((2, nz) + side_block[1:], BF16),
        pltpu.VMEM((2, nz) + side_block[1:], BF16),
        dma((6,)),
    ]
    gather = [dma((nz,)), dma((nz,)), dma((half_n,)), dma((2, half_n))]
    exchange = [dma((half_n,)), dma((half_n,))]
    staged = [dma((nz,)), dma((nz,)), dma((nz,)), dma((nz,))]
    scratch += gather + gather
    scratch += [dma((5,)), dma((5,))]
    scratch += exchange + exchange
    scratch += [dma((n,)), dma((n,))]
    scratch += staged + gather + gather + [dma((2, nz))] * 4
    out = pl.pallas_call(
        functools.partial(kernel, n),
        out_shape=jax.ShapeDtypeStruct((2, cap, D), BF16),
        in_specs=[vmem] * 4 + [anywhere] * 3 + [vmem] * 3 + [anywhere] * 3,
        out_specs=vmem,
        scratch_shapes=scratch,
        compiler_params=pltpu.CompilerParams(
            collective_id=0, has_side_effects=True, vmem_limit_bytes=60 * 2**20
        ),
    )(
        lengths.reshape(1, keys.shape[0]),
        owner_counts.reshape(1, n),
        row_order.reshape(1, rows),
        queries,
        keys,
        values,
        residual,
        expert_ids.T,
        route_weights.T,
        norm_gain.reshape(1, D),
        out_weight,
        gate_up,
        expert_down,
    )
    return out[0], out[1]


def solution(mesh):
    placed = (
        P(("groups", "ctx"), None),
        P("groups", "ctx", None),
        P("groups", "ctx", None),
        P("groups"),
        P("groups"),
        P("groups"),
        P(("groups", "ctx"), None),
        P("ctx", None),
        P(),
        P(("groups", "ctx"), None),
        P(("groups", "ctx"), None),
        P("ctx", None, None),
        P("ctx", None, None),
    )
    return jax.shard_map(
        body,
        mesh=mesh,
        in_specs=placed,
        out_specs=(P(("groups", "ctx"), None), P(("groups", "ctx"), None)),
        check_vma=False,
    )
```

```python
import functools

import jax
import jax.numpy as jnp
from jax import lax
from jax.experimental import pallas as pl
from jax.experimental.pallas import tpu as pltpu
from jax.sharding import PartitionSpec as P

D = 2048
HQ = 16
KVH = 2
HD = 128
EFF = 768
TOPK = 8
STRETCH = 128
GROUPS = HQ // KVH
LANES = 128
LOG2E = 1.4426950408889634
F32 = jnp.float32
BF16 = jnp.bfloat16
MESH = pl.DeviceIdType.MESH


def dot(a, b, ca, cb):
    return lax.dot_general(a, b, (((ca,), (cb,)), ((), ())), preferred_element_type=F32)


def kernel(
    n,
    lengths,
    counts_ref,
    order_ref,
    q_ref,
    keys_hbm,
    values_hbm,
    residual_hbm,
    ids_ref,
    route_ref,
    gain_ref,
    ow_hbm,
    gu_hbm,
    down_hbm,
    out,
    keys_ref,
    values_ref,
    ow,
    gu,
    down,
    q_all,
    c_all,
    mix_snd,
    st_snd,
    mix_rcv,
    st_rcv,
    m_snd,
    s_snd,
    m_in,
    s_in,
    a_snd,
    a_in,
    p_snd,
    p_rcv,
    p_mid,
    p_in,
    p_yin,
    r_all,
    n_all,
    x_buf,
    str_buf,
    hid,
    e_snd,
    e_rcv,
    e_mid,
    e_in,
    e_yin,
    w_sem,
    q_s,
    q_y,
    q_f,
    q_r,
    c_s,
    c_y,
    c_f,
    c_r,
    pair_s,
    pair_r,
    m_s,
    m_r,
    s_s,
    s_r,
    a_s,
    a_r,
    p_s,
    p_y,
    p_r,
    p_yr,
    r_s,
    r_y,
    r_f,
    r_r,
    n_s,
    n_y,
    n_f,
    n_r,
    e_s,
    e_y,
    e_r,
    e_yr,
):
    half_n = n // 2
    home = q_ref.shape[0]
    rows = n * home
    cap = residual_hbm.shape[0]
    slots = n * cap
    chunk = ow.shape[0]
    span = keys_ref.shape[1]
    requests = keys_ref.shape[0]
    me = lax.axis_index("ctx")
    par = lax.rem(me, 2)
    half = me // 2
    other = 1 - par
    sib = half * 2 + other

    ny = 2 if half_n % 2 == 0 else 1
    nz = half_n // ny
    z, y = half // ny, lax.rem(half, ny)

    def peer(k):
        return lax.rem(half + k, half_n)

    def remote(src, dst, ss, rs, dev):
        return pltpu.make_async_remote_copy(
            src_ref=src, dst_ref=dst, send_sem=ss, recv_sem=rs,
            device_id={"ctx": dev}, device_id_type=MESH,
        )

    def each(lo, hi, f):
        def step(k, c):
            f(k)
            return c
        lax.fori_loop(lo, hi, step, 0)

    loads = [
        pltpu.make_async_copy(ow_hbm, ow, w_sem.at[0]),
        pltpu.make_async_copy(gu_hbm.at[0], gu, w_sem.at[1]),
        pltpu.make_async_copy(down_hbm.at[0], down, w_sem.at[2]),
    ]

    cache = [
        pltpu.make_async_copy(keys_hbm, keys_ref, w_sem.at[3]),
        pltpu.make_async_copy(values_hbm, values_ref, w_sem.at[4]),
    ]
    load_res = pltpu.make_async_copy(residual_hbm, r_all.at[par, half], w_sem.at[5])
    load_res.start()
    for load in cache:
        load.start()

    barrier = pltpu.get_barrier_semaphore()
    each(1, n, lambda k: pl.semaphore_signal(
        barrier, inc=1, device_id={"ctx": lax.rem(me + k, n)}, device_id_type=MESH))

    qf = q_ref[...].astype(F32)
    width = GROUPS * HD
    q_all[par, half] = jnp.concatenate(
        [qf[:, v * width:(v + 1) * width] for v in range(KVH)], axis=0).astype(BF16)

    counts = counts_ref[...].astype(F32)

    def slot_info(index, owner, place):
        lane = lax.broadcasted_iota(jnp.int32, (index, n), 1)
        start = jnp.sum(jnp.where(lane < owner, counts, 0.0), axis=1, keepdims=True)
        held = jnp.sum(jnp.where(lane == owner, counts, 0.0), axis=1, keepdims=True)
        return start, place.astype(F32) < held

    own_place = lax.broadcasted_iota(jnp.int32, (cap, 1), 0)
    _, own_valid = slot_info(cap, jnp.zeros((cap, 1), jnp.int32) + me, own_place)

    def upright(flat):
        return jnp.concatenate([flat, jnp.zeros((TOPK, LANES - cap), F32)], axis=1).T[:cap]

    ids = upright(ids_ref[...].astype(F32)).astype(jnp.int32)
    route = upright(route_ref[...])
    route = route / jnp.sum(route, axis=1, keepdims=True)
    expert_lane = lax.broadcasted_iota(jnp.int32, (cap, c_all.shape[-1]), 1)
    mixw = jnp.zeros((cap, c_all.shape[-1]), F32)
    for k in range(TOPK):
        mixw = mixw + jnp.where(expert_lane == ids[:, k:k + 1], route[:, k:k + 1], 0.0)
    c_all[par, half] = jnp.where(own_valid, mixw, 0.0)

    pl.semaphore_wait(barrier, n - 1)

    def z_to(k):
        k = lax.rem(k, nz)
        if nz & (nz - 1):
            return lax.rem(z + k, nz)
        to, bit = 0, 1
        while bit < nz:
            to = to + lax.rem(z // bit + k // bit, 2) * bit
            bit = bit * 2
        return to

    def z_peer(k):
        return z_to(k) * ny + y

    def y_peer(k):
        return z_to(k) * ny + (ny - 1 - y)

    z_own_y = z * ny + (ny - 1 - y)

    def block_copy(buf, pa, h, sem, rs, dev):
        block = buf.at[pa, h]
        return remote(block, block, sem, rs.at[pa, h], dev)

    def gather_start(buf, sems):
        ss, ys, fs, rs = sems
        each(1, nz, lambda k: block_copy(
            buf, par, half, ss.at[k], rs, z_peer(k) * 2 + par).start())
        if ny > 1:
            block_copy(buf, par, half, ys.at[0], rs, z_own_y * 2 + par).start()
        block_copy(buf, par, half, ss.at[0], rs, sib).start()

    def pass_on(buf, sems, h):
        ss, ys, fs, rs = sems
        block_copy(buf, par, h, ss.at[0], rs, sib).wait_recv()
        block_copy(buf, par, h, fs.at[h], rs, sib).start()

    def gather_z(buf, sems):
        ss, ys, fs, rs = sems
        if ny > 1:
            pass_on(buf, sems, z_own_y)

        def step(k):
            h = z_peer(k)
            pass_on(buf, sems, h)
            if ny > 1:
                block_copy(buf, par, h, ys.at[k], rs, z_own_y * 2 + par).start()
        each(1, nz, step)

    def gather_y(buf, sems):
        if ny > 1:
            each(1, nz, lambda k: pass_on(buf, sems, y_peer(k)))

    def gather_finish(buf, sems):
        ss, ys, fs, rs = sems
        each(0, half_n, lambda h: block_copy(
            buf, other, h, ss.at[0], rs, sib).wait_recv())

    def gather_drain(buf, sems):
        ss, ys, fs, rs = sems
        each(0, nz, lambda k: block_copy(buf, par, half, ss.at[k], rs, sib).wait_send())
        if ny > 1:
            each(0, nz, lambda k: block_copy(buf, par, half, ys.at[k], rs, sib).wait_send())
        each(1, half_n, lambda k: block_copy(
            buf, par, peer(k), fs.at[peer(k)], rs, sib).wait_send())

    q_g = (q_s, q_y, q_f, q_r)
    c_g = (c_s, c_y, c_f, c_r)
    r_g = (r_s, r_y, r_f, r_r)
    n_g = (n_s, n_y, n_f, n_r)
    gather_start(q_all, q_g)
    for load in loads:
        load.start()

    index = lax.broadcasted_iota(jnp.int32, (slots, 1), 0)
    block_of = index // cap
    owner = lax.rem(block_of, half_n) * 2 + block_of // half_n
    place = lax.rem(index, cap)
    start, filled = slot_info(slots, owner, place)
    at = start + place.astype(F32)
    row_lane = lax.broadcasted_iota(jnp.int32, (slots, rows), 1).astype(F32)
    order = order_ref[...].astype(F32)
    row_of = jnp.sum(jnp.where(row_lane == at, order, 0.0), axis=1, keepdims=True)
    row_of = jnp.where(filled, row_of, -1.0)
    pick = (row_lane == row_of).astype(BF16)
    lane = lax.broadcasted_iota(jnp.int32, (slots, rows), 1)
    block_lane = lane // home
    device_lane = lax.rem(block_lane, half_n) * 2 + block_lane // half_n
    row_lane = (device_lane * home + lax.rem(lane, home)).astype(F32)
    pick_par = (row_lane == row_of).astype(BF16)
    own_lane = me * home + lax.broadcasted_iota(jnp.int32, (slots, LANES), 1)
    pick_own = (own_lane.astype(F32) == row_of).astype(BF16)

    gather_z(q_all, q_g)
    gather_y(q_all, q_g)
    gather_finish(q_all, q_g)
    gather_start(c_all, c_g)
    load_res.wait()
    gather_start(r_all, r_g)
    for load in cache:
        load.wait()

    first_key = me * span
    per_head = HD // chunk
    pair = 2
    for request in range(requests):
        length = lengths[:, request:request + 1]
        blocks = STRETCH // home
        lo = request * blocks
        q_req = jnp.stack(
            [q_all[(lo + b) % 2, (lo + b) // 2]
             for b in range(blocks)], axis=0).astype(F32)
        q_req = q_req.reshape(blocks, KVH, home, width)
        key_pos = first_key + lax.broadcasted_iota(jnp.int32, (span, pair * STRETCH), 0)
        row_pos = length - STRETCH + lax.rem(
            lax.broadcasted_iota(jnp.int32, (span, pair * STRETCH), 1), STRETCH)
        allowed = key_pos <= row_pos
        for v in range(KVH):
            key_v = keys_ref[request, :, v * HD:(v + 1) * HD]
            val_v = values_ref[request, :, v * HD:(v + 1) * HD]
            val_t = val_v.astype(F32).T.astype(BF16)
            q_v = q_req[:, v].reshape(STRETCH, width)
            for g in range(0, GROUPS, pair):
                q_pair = jnp.concatenate(
                    [q_v[:, (g + i) * HD:(g + i + 1) * HD] for i in range(pair)],
                    axis=0).astype(BF16)
                scores = jnp.where(allowed, dot(key_v, q_pair, 1, 1), -1e30)
                top = jnp.max(scores, axis=0, keepdims=True)
                some = top > -1e29
                weights = jnp.exp2((scores - top) * (HD ** (-0.5) * LOG2E))
                total = jnp.where(some, jnp.sum(weights, axis=0, keepdims=True), 0.0)
                mixed = dot(val_t, weights.astype(BF16), 1, 0)
                mixed = jnp.where(some, mixed, 0.0).astype(BF16)
                top = jnp.where(some, top * HD ** (-0.5), -1e30)
                for i in range(pair):
                    head = v * GROUPS + g + i
                    cols = slice(request * STRETCH, (request + 1) * STRETCH)
                    take = slice(i * STRETCH, (i + 1) * STRETCH)
                    for c in range(per_head):
                        j = head * per_head + c
                        mix_snd[j % 2, j // 2, :, cols] = mixed[c * chunk:(c + 1) * chunk, take]
                        st_snd[j % 2, 0, j // 2:j // 2 + 1, cols] = top[:, take]
                        st_snd[j % 2, 1, j // 2:j // 2 + 1, cols] = total[:, take]

    x_mix = remote(mix_snd.at[other], mix_rcv, pair_s.at[0], pair_r.at[0], sib)
    x_st = remote(st_snd.at[other], st_rcv, pair_s.at[1], pair_r.at[1], sib)
    x_st.start()
    x_mix.start()
    gather_z(c_all, c_g)
    x_st.wait()
    x_mix.wait()
    top_a, top_b = st_snd[par, 0], st_rcv[0]
    best = jnp.maximum(top_a, top_b)
    fac_a, fac_b = jnp.exp(top_a - best), jnp.exp(top_b - best)
    total = st_snd[par, 1] * fac_a + st_rcv[1] * fac_b
    for q in range(half_n):
        s_snd[q, 0:1] = best[q:q + 1]
        s_snd[q, 1:2] = total[q:q + 1]
        m_snd[q] = (mix_snd[par, q].astype(F32) * fac_a[q:q + 1]
                    + mix_rcv[q].astype(F32) * fac_b[q:q + 1]).astype(BF16)

    def part_copies(k):
        p = peer(k)
        dev = p * 2 + par
        return (
            remote(s_snd.at[p], s_in.at[half], s_s.at[k], s_r.at[half], dev),
            remote(m_snd.at[p], m_in.at[half], m_s.at[k], m_r.at[half], dev),
        )

    def start_parts(k):
        for c in part_copies(k):
            c.start()

    each(1, half_n, start_parts)
    gather_y(c_all, c_g)
    s_in[half, 0:2] = s_snd[half, 0:2]
    m_in[half] = m_snd[half]
    loads[0].wait()

    def wait_parts(k):
        p = peer(k)
        remote(s_snd.at[p], s_in.at[p], s_s.at[k], s_r.at[p], sib).wait_recv()
        remote(m_snd.at[p], m_in.at[p], m_s.at[k], m_r.at[p], sib).wait_recv()

    each(1, half_n, wait_parts)
    gather_z(r_all, r_g)
    best = s_in[0, 0:1]
    for q in range(1, half_n):
        best = jnp.maximum(best, s_in[q, 0:1])
    denom = jnp.zeros_like(best)
    numer = jnp.zeros((chunk, rows), F32)
    for q in range(half_n):
        factor = jnp.exp(s_in[q, 0:1] - best)
        denom = denom + factor * s_in[q, 1:2]
        numer = numer + m_in[q].astype(F32) * factor
    attn = (numer / denom).astype(BF16)

    a_slots = dot(pick, attn, 1, 1).astype(BF16)
    a_snd[...] = a_slots.reshape(2, half_n, cap, chunk)

    def attn_copy(k):
        to = lax.rem(me + k, n)
        return remote(a_snd.at[lax.rem(to, 2), to // 2], a_in.at[me],
                      a_s.at[k], a_r.at[me], to)

    part = dot(attn, ow[...], 0, 0)
    wide = D // 2
    for d in range(n):
        own = part[d * home:(d + 1) * home]
        p_snd[d % 2, d // 2] = jnp.concatenate(
            [own[:, :wide], own[:, wide:]], axis=0).astype(BF16)
    x_p = remote(p_snd.at[other], p_rcv, pair_s.at[2], pair_r.at[2], sib)
    x_p.start()
    gather_y(r_all, r_g)
    x_p.wait()

    def spread_y(mine, got, mid, into, yin, ss, ys, rs, yr):
        if ny > 1:
            def step_y(k):
                h = y_peer(nz - k)
                to = h // ny
                mid[h] = (mine[par, h].astype(F32) + got[h].astype(F32)).astype(BF16)
                remote(mid.at[h], yin.at[to], ys.at[k - 1], yr.at[to],
                       z_own_y * 2 + par).start()
            each(1, nz + 1, step_y)

    def spread_z(mine, got, mid, into, yin, ss, ys, rs, yr):
        def step(k):
            h = z_peer(nz - k)
            total = mine[par, h].astype(F32) + got[h].astype(F32)
            if ny > 1:
                to = h // ny
                remote(mid.at[h], yin.at[to], ss.at[k], yr.at[to], sib).wait_recv()
                total = total + yin[to].astype(F32)
            mid[h] = total.astype(BF16)
            remote(mid.at[h], into.at[z], ss.at[k], rs.at[z], h * 2 + par).start()
        each(1, nz, step)

    def collect(mine, got, mid, into, yin, ss, ys, rs, yr):
        total = mine[par, half].astype(F32) + got[half].astype(F32)
        if ny > 1:
            remote(mid.at[0], yin.at[z], ss.at[0], yr.at[z], sib).wait_recv()
            total = total + yin[z].astype(F32)

        def step(k, total):
            at_z = lax.rem(z - k + nz, nz)
            remote(mid.at[0], into.at[at_z], ss.at[k], rs.at[at_z], sib).wait_recv()
            return total + into[at_z].astype(F32)
        return lax.fori_loop(1, nz, step, total)

    def drain_spread(mid, into, yin, ss, ys, rs, yr):
        each(1, nz, lambda k: remote(
            mid.at[0], into.at[0], ss.at[k], rs.at[0], sib).wait_send())
        if ny > 1:
            each(0, nz, lambda k: remote(
                mid.at[0], yin.at[0], ys.at[k], yr.at[0], sib).wait_send())

    p_x = (p_mid, p_in, p_yin, p_s, p_y, p_r, p_yr)
    e_x = [[ref.at[i] for ref in (
        e_snd, e_rcv, e_mid, e_in, e_yin, e_s, e_y, e_r, e_yr)] for i in range(2)]
    spread_y(p_snd, p_rcv, *p_x)
    spread_z(p_snd, p_rcv, *p_x)

    gather_finish(r_all, r_g)
    held = dot(pick_own, r_all[...].reshape(slots, D), 0, 0)[:home]
    held = jnp.concatenate([held[:, :wide], held[:, wide:]], axis=0)
    projected = collect(p_snd, p_rcv, *p_x)
    stream = (held + projected).astype(BF16).astype(F32)
    square = jnp.sum(stream * stream, axis=1, keepdims=True)
    scale = lax.rsqrt((square[:home] + square[home:]) / D + 1e-06)
    gain = gain_ref[...]
    gain = jnp.concatenate(
        [jnp.broadcast_to(gain[:, :wide], (home, wide)),
         jnp.broadcast_to(gain[:, wide:], (home, wide))], axis=0)
    normed = stream * jnp.concatenate([scale, scale], axis=0) * gain
    n_all[par, half] = normed.astype(BF16)
    gather_start(n_all, n_g)
    blank = jnp.zeros((LANES - home, D), F32)
    str_buf[...] = jnp.concatenate(
        [jnp.concatenate([stream[:home], stream[home:]], axis=1), blank], axis=0).astype(BF16)
    gather_finish(c_all, c_g)
    loads[1].wait()
    loads[2].wait()
    gather_z(n_all, n_g)
    gather_y(n_all, n_g)

    def repack(parity):
        halves = n_all[parity].astype(F32).reshape(half_n, 2, home, wide)
        x_buf[parity, :, :wide] = halves[:, 0].reshape(rows // 2, wide).astype(BF16)
        x_buf[parity, :, wide:] = halves[:, 1].reshape(rows // 2, wide).astype(BF16)

    repack(par)
    gather_finish(n_all, n_g)
    repack(other)

    lane = lax.broadcasted_iota(jnp.int32, (slots, c_all.shape[-1]), 1)
    tile = 256
    each(1, n, lambda k: attn_copy(k).start())

    x = x_buf.reshape(rows, D)

    def up(t, c):
        lo = pl.multiple_of(t * tile, tile)
        gate = dot(x[...], gu[:, pl.ds(lo, tile)], 1, 0)
        lift = dot(x[...], gu[:, pl.ds(EFF + lo, tile)], 1, 0)
        hid[:, pl.ds(lo, tile)] = (gate / (1.0 + jnp.exp(-gate)) * lift).astype(BF16)
        return c
    lax.fori_loop(0, EFF // tile, up, 0)
    routes = c_all[...].reshape(slots, c_all.shape[-1])
    weight = jnp.sum(jnp.where(lane == me, routes, 0.0), axis=1, keepdims=True)

    side = D // 2

    def lower(i, first, last):
        def step(t, c):
            lo = pl.multiple_of(t * tile, tile)
            cols = pl.ds(pl.multiple_of(i * side + lo, tile), tile)
            result = dot(hid[...], down[:, cols], 1, 0).astype(BF16)
            part = dot(pick_par, result, 1, 0) * weight
            part = part + dot(pick_own, str_buf[:, cols], 1, 0)
            e_snd[i, :, :, :, pl.ds(lo, tile)] = part.astype(BF16).reshape(
                2, half_n, cap, tile)
            return c
        lax.fori_loop(first, last, step, 0)

    x_e = [remote(e_snd.at[i, other], e_rcv.at[i], pair_s.at[3 + i], pair_r.at[3 + i], sib)
           for i in range(2)]
    tiles = side // tile
    lower(0, 0, tiles)
    x_e[0].start()
    lower(1, 0, tiles // 2)
    x_e[0].wait()
    spread_y(*e_x[0])
    lower(1, tiles // 2, tiles)
    x_e[1].start()
    x_e[1].wait()
    spread_y(*e_x[1])
    spread_z(*e_x[0])
    spread_z(*e_x[1])

    a_in[me] = a_snd[par, half]

    def wait_attn(k):
        at_k = lax.rem(me + k, n)
        remote(a_snd.at[0, 0], a_in.at[at_k], a_s.at[k], a_r.at[at_k], sib).wait_recv()

    each(1, n, wait_attn)
    out[0] = jnp.concatenate([a_in[j] for j in range(n)], axis=1)

    moe = jnp.concatenate([collect(*e_x[i]) for i in range(2)], axis=1)
    out[1] = jnp.where(own_valid, moe, 0.0).astype(BF16)

    def drain(k):
        for c in part_copies(k):
            c.wait_send()

    each(1, half_n, drain)
    drain_spread(*p_x)
    drain_spread(*e_x[0][2:])
    drain_spread(*e_x[1][2:])
    gather_drain(q_all, q_g)
    gather_drain(c_all, c_g)
    gather_drain(r_all, r_g)
    gather_drain(n_all, n_g)
    each(1, n, lambda k: attn_copy(k).wait_send())


def body(
    queries,
    keys,
    values,
    lengths,
    owner_counts,
    row_order,
    residual,
    out_weight,
    norm_gain,
    expert_ids,
    route_weights,
    gate_up,
    expert_down,
):
    n = lax.axis_size("ctx")
    half_n = n // 2
    home = queries.shape[0]
    rows = n * home
    cap = residual.shape[0]
    chunk = out_weight.shape[0]
    lanes = -(-n // LANES) * LANES
    vmem = pl.BlockSpec(memory_space=pltpu.VMEM)
    anywhere = pl.BlockSpec(memory_space=pl.ANY)
    dma = pltpu.SemaphoreType.DMA
    slot_block = (half_n, cap, D)
    ny = 2 if half_n % 2 == 0 else 1
    nz = half_n // ny
    side_block = (half_n, cap, D // 2)
    row_block = (half_n, 2 * home, D // 2)
    scratch = [
        pltpu.VMEM(keys.shape, BF16),
        pltpu.VMEM(values.shape, BF16),
        pltpu.VMEM(out_weight.shape, BF16),
        pltpu.VMEM(gate_up.shape[1:], BF16),
        pltpu.VMEM(expert_down.shape[1:], BF16),
        pltpu.VMEM((2, half_n, KVH * home, GROUPS * HD), BF16),
        pltpu.VMEM((2, half_n, cap, lanes), F32),
        pltpu.VMEM((2, half_n, chunk, rows), BF16),
        pltpu.VMEM((2, 2, half_n, rows), F32),
        pltpu.VMEM((half_n, chunk, rows), BF16),
        pltpu.VMEM((2, half_n, rows), F32),
        pltpu.VMEM((half_n, chunk, rows), BF16),
        pltpu.VMEM((half_n, 8, rows), F32),
        pltpu.VMEM((half_n, chunk, rows), BF16),
        pltpu.VMEM((half_n, 8, rows), F32),
        pltpu.VMEM((2, half_n, cap, chunk), BF16),
        pltpu.VMEM((n, cap, chunk), BF16),
        pltpu.VMEM((2,) + row_block, BF16),
        pltpu.VMEM(row_block, BF16),
        pltpu.VMEM(row_block, BF16),
        pltpu.VMEM((nz,) + row_block[1:], BF16),
        pltpu.VMEM((nz,) + row_block[1:], BF16),
        pltpu.VMEM((2,) + slot_block, BF16),
        pltpu.VMEM((2,) + row_block, BF16),
        pltpu.VMEM((2, rows // 2, D), BF16),
        pltpu.VMEM((LANES, D), BF16),
        pltpu.VMEM((rows, EFF), BF16),
        pltpu.VMEM((2, 2) + side_block, BF16),
        pltpu.VMEM((2,) + side_block, BF16),
        pltpu.VMEM((2,) + side_block, BF16),
        pltpu.VMEM((2, nz) + side_block[1:], BF16),
        pltpu.VMEM((2, nz) + side_block[1:], BF16),
        dma((6,)),
    ]
    gather = [dma((nz,)), dma((nz,)), dma((half_n,)), dma((2, half_n))]
    exchange = [dma((half_n,)), dma((half_n,))]
    staged = [dma((nz,)), dma((nz,)), dma((nz,)), dma((nz,))]
    scratch += gather + gather
    scratch += [dma((5,)), dma((5,))]
    scratch += exchange + exchange
    scratch += [dma((n,)), dma((n,))]
    scratch += staged + gather + gather + [dma((2, nz))] * 4
    out = pl.pallas_call(
        functools.partial(kernel, n),
        out_shape=jax.ShapeDtypeStruct((2, cap, D), BF16),
        in_specs=[vmem] * 4 + [anywhere] * 3 + [vmem] * 3 + [anywhere] * 3,
        out_specs=vmem,
        scratch_shapes=scratch,
        compiler_params=pltpu.CompilerParams(
            collective_id=0, has_side_effects=True, vmem_limit_bytes=60 * 2**20
        ),
    )(
        lengths.reshape(1, keys.shape[0]),
        owner_counts.reshape(1, n),
        row_order.reshape(1, rows),
        queries,
        keys,
        values,
        residual,
        expert_ids.T,
        route_weights.T,
        norm_gain.reshape(1, D),
        out_weight,
        gate_up,
        expert_down,
    )
    return out[0], out[1]


def solution(mesh):
    placed = (
        P(("groups", "ctx"), None),
        P("groups", "ctx", None),
        P("groups", "ctx", None),
        P("groups"),
        P("groups"),
        P("groups"),
        P(("groups", "ctx"), None),
        P("ctx", None),
        P(),
        P(("groups", "ctx"), None),
        P(("groups", "ctx"), None),
        P("ctx", None, None),
        P("ctx", None, None),
    )
    return jax.shard_map(
        body,
        mesh=mesh,
        in_specs=placed,
        out_specs=(P(("groups", "ctx"), None), P(("groups", "ctx"), None)),
        check_vma=False,
    )
```
